256 devices in a mesh: gx: 16 (over y, x_hi, core), gy: 16 (over x_lo, z).
Axes of the slice: x: 4 (x_hi: 2, x_lo: 2; x = x_hi * 2 + x_lo), y: 4, z: 8, core: 2. Of those that a mesh axis runs over, the one named last changes fastest.
Arguments:
- tokens: bfloat16 [128, 128, 1536], P('gx', 'gy'), may hold values from -6 to 6
- cotangent: bfloat16 [128, 128, 1536], P('gx', 'gy'), may hold values from -6 to 6
- qkv_weight: bfloat16 [192, 576], replicated, may hold values from -4 to 4
- qkv_bias: float32 [576], replicated, may hold values from -4 to 4
- proj_weight: bfloat16 [192, 192], replicated, may hold values from -0.4375 to 0.4375
- proj_bias: float32 [192], replicated, may hold values from -4 to 4
- fc1_weight: bfloat16 [192, 768], replicated, may hold values from -0.4375 to 0.4375
- fc1_bias: float32 [768], replicated, may hold values from -4 to 4
- fc2_weight: bfloat16 [768, 192], replicated, may hold values from -0.21875 to 0.21875
- norm1_gain: float32 [192], replicated, may hold values from 0.1 to 1.9
- norm1_bias: float32 [192], replicated, may hold values from -4 to 4
- norm2_gain: float32 [192], replicated, may hold values from 0.1 to 1.9
- norm2_bias: float32 [192], replicated, may hold values from -4 to 4
Outputs:
- grad_tokens: bfloat16 [128, 128, 1536], P('gx', 'gy')
- grad_qkv: float32 [192, 576], replicated
- grad_proj: float32 [192, 192], replicated
- grad_fc1: float32 [192, 768], replicated
- grad_fc2: float32 [768, 192], replicated
- grad_vectors: float32 [2304], replicated
The draws below stay inside these ranges and needn't reach their ends.
All inputs are finite; a program needn't handle non-finite values.
Results may differ from the reference program's by a relative error of at most 0.017.
The reference program's roundings to bfloat16 on the way count: a program that leaves them out, or rounds other values in their place, can miss the bound.
Values may be sent and summed in bfloat16 or wider, within the bound.
No kernel may reach another device: no remote copies, remote signals or barrier semaphores. Data moves between devices by JAX's collectives and lax.ppermute only.
A program may use at most 64 MiB of HBM per device.

```python
from functools import partial
import jax
import jax.numpy as jnp
from jax import lax

WIDTH = 192
HEADS = 6
HEAD_DIM = 32
MLP_WIDTH = 768
WIN = 8
DEPTH = 8
NX = 128
NY = 128
TOKENS = 131072


def draw_qkv_weight(key, part):
    key = jax.random.fold_in(key, 7)
    base_key = jax.random.fold_in(key, 0)
    spread = 1.5 * WIDTH ** (-0.5)
    weight = jax.random.normal(base_key, (WIDTH, 3 * WIDTH), jnp.float32) * spread
    weight = jnp.clip(weight, -6.0 * spread, 6.0 * spread)
    return jnp.clip(weight, -4.0, 4.0).astype(jnp.bfloat16)


def level_of(own_key, shape, pieces, low, top_value):
    def one(axis_at, shards_of):
        heights = jax.random.uniform(jax.random.fold_in(jax.random.fold_in(own_key, 6), axis_at), (shards_of,), jnp.float32, low / len(pieces), top_value / len(pieces))
        return jnp.repeat(jnp.exp(heights), shape[axis_at] // shards_of).reshape((-1,) + (1,) * (len(shape) - axis_at - 1))

    level = one(*pieces[0])
    for cut in pieces[1:]:
        level = level * one(*cut)
    return level


def bell_draw(rng, shape, scale, limit, pieces=(), kind=jnp.bfloat16):
    drawn = scale * jax.random.normal(rng, shape, jnp.float32)
    if pieces:
        drawn = drawn * level_of(rng, shape, pieces, -0.22, 0.18)
    return jnp.clip(drawn, -limit, limit).astype(kind)


def setup_inputs(seed: int = 0) -> dict:
    key_list = jax.random.split(jax.random.key(seed), 14)
    tokens = bell_draw(key_list[0], (NX, NY, DEPTH * WIDTH), 1.0, 6.0, ((0, 16), (1, 16)))
    cotangent = bell_draw(key_list[1], (NX, NY, DEPTH * WIDTH), 1.0, 6.0, ((0, 16), (1, 16)))
    qkv_weight = draw_qkv_weight(jax.random.fold_in(key_list[13], 71), 0)
    qkv_bias = bell_draw(key_list[3], (3 * WIDTH,), 0.3, 4.0, (), jnp.float32)
    proj_weight = bell_draw(key_list[4], (WIDTH, WIDTH), WIDTH ** -0.5, 0.4375)
    proj_bias = bell_draw(key_list[5], (WIDTH,), 0.3, 4.0, (), jnp.float32)
    fc1_weight = bell_draw(key_list[6], (WIDTH, MLP_WIDTH), WIDTH ** -0.5, 0.4375)
    fc1_bias = bell_draw(key_list[7], (MLP_WIDTH,), 0.3, 4.0, (), jnp.float32)
    fc2_weight = bell_draw(key_list[8], (MLP_WIDTH, WIDTH), MLP_WIDTH ** -0.5, 0.21875)
    norm1_gain = jnp.clip(1.0 + 0.18 * jax.random.normal(key_list[9], (WIDTH,), jnp.float32), 0.1, 1.9)
    norm1_bias = bell_draw(key_list[10], (WIDTH,), 0.3, 4.0, (), jnp.float32)
    norm2_gain = jnp.clip(1.0 + 0.18 * jax.random.normal(key_list[11], (WIDTH,), jnp.float32), 0.1, 1.9)
    norm2_bias = bell_draw(key_list[12], (WIDTH,), 0.3, 4.0, (), jnp.float32)
    return {"tokens": tokens, "cotangent": cotangent, "qkv_weight": qkv_weight, "qkv_bias": qkv_bias, "proj_weight": proj_weight, "proj_bias": proj_bias, "fc1_weight": fc1_weight, "fc1_bias": fc1_bias, "fc2_weight": fc2_weight, "norm1_gain": norm1_gain, "norm1_bias": norm1_bias, "norm2_gain": norm2_gain, "norm2_bias": norm2_bias}


eps = 1e-05

def matmul(left_side, right_side):
    return jnp.dot(left_side, right_side, preferred_element_type=jnp.float32)

def rounded(value_full):
    return lax.optimization_barrier(value_full.astype(jnp.bfloat16)).astype(jnp.float32)

def norm_forward(inputs, gain_vector, bias_vector):
    centred = inputs - lax.optimization_barrier(jnp.mean(inputs, axis=-1, keepdims=True))
    inverse = lax.rsqrt(lax.optimization_barrier(jnp.mean(centred * centred, axis=-1, keepdims=True)) + eps)
    normed = centred * inverse
    return ((normed * gain_vector + bias_vector).astype(jnp.bfloat16), normed, inverse)

def norm_backward(incoming, normed, inverse, gain_vector):
    scaled = incoming * gain_vector
    centre = lax.optimization_barrier(jnp.mean(scaled, axis=-1, keepdims=True))
    projection = lax.optimization_barrier(jnp.mean(scaled * normed, axis=-1, keepdims=True))
    result = inverse * (scaled - centre - normed * projection)
    return (result, lax.optimization_barrier(jnp.sum(incoming * normed, axis=0)), lax.optimization_barrier(jnp.sum(incoming, axis=0)))

def gelu_parts(hidden_pre):
    normal_cdf = 0.5 * (1.0 + lax.erf(hidden_pre * 0.7071067811865476))
    normal_pdf = jnp.exp(-0.5 * hidden_pre * hidden_pre) * 0.3989422804014327
    return (hidden_pre * normal_cdf, normal_cdf + hidden_pre * normal_pdf)

def window_pass(weights, running, inputs):
    qkv_weight, qkv_bias, proj_weight, proj_bias, fc1_weight, fc1_bias, fc2_weight, norm1_gain, norm1_bias, norm2_gain, norm2_bias = weights
    tok_rows, cot_rows = inputs
    row_count = tok_rows.shape[0]
    features = WIDTH
    query_scale = HEAD_DIM ** (-0.5)
    tokens32 = tok_rows.astype(jnp.float32)
    attn_in, hat_one, inv_one = norm_forward(tokens32, norm1_gain, norm1_bias)
    projected = matmul(attn_in, qkv_weight) + qkv_bias
    queries = rounded(projected[:, :features] * query_scale).reshape(row_count, HEADS, HEAD_DIM)
    key_heads = rounded(projected[:, features:2 * features]).reshape(row_count, HEADS, HEAD_DIM)
    values = rounded(projected[:, 2 * features:]).reshape(row_count, HEADS, HEAD_DIM)
    scores = jnp.einsum('qhd,khd->hqk', queries, key_heads)
    attention = jax.nn.softmax(scores, axis=-1)
    attention_b = rounded(attention)
    blended = jnp.einsum('hqk,khd->qhd', attention_b, values).reshape(row_count, features).astype(jnp.bfloat16)
    branch = (matmul(blended, proj_weight) + proj_bias).astype(jnp.bfloat16)
    residual = tokens32 + branch.astype(jnp.float32)
    mlp_in, hat_two, inv_two = norm_forward(residual, norm2_gain, norm2_bias)
    hidden_pre = matmul(mlp_in, fc1_weight) + fc1_bias
    active, derivative = gelu_parts(hidden_pre)
    active_b = active.astype(jnp.bfloat16)
    grad_fc2 = matmul(active_b.T, cot_rows)
    grad_pre = matmul(cot_rows, fc2_weight.T) * derivative
    grad_pre_b = grad_pre.astype(jnp.bfloat16)
    grad_fc1 = matmul(mlp_in.T, grad_pre_b)
    grad_mlp_in = matmul(grad_pre_b, fc1_weight.T)
    grad_norm2, gain_two, bias_two = norm_backward(grad_mlp_in, hat_two, inv_two, norm2_gain)
    grad_resid = cot_rows.astype(jnp.float32) + grad_norm2
    grad_branch = grad_resid.astype(jnp.bfloat16)
    grad_proj = matmul(blended.T, grad_branch)
    grad_proj_bias = lax.optimization_barrier(jnp.sum(grad_branch.astype(jnp.float32), axis=0))
    grad_blend = rounded(matmul(grad_branch, proj_weight.T)).reshape(row_count, HEADS, HEAD_DIM)
    grad_values = jnp.einsum('hqk,qhd->khd', attention_b, grad_blend)
    grad_attention = jnp.einsum('qhd,khd->hqk', grad_blend, values)
    grad_scores = rounded(attention * (grad_attention - lax.optimization_barrier(jnp.sum(grad_attention * attention, axis=-1, keepdims=True))))
    grad_queries = jnp.einsum('hqk,khd->qhd', grad_scores, key_heads) * query_scale
    grad_keys = jnp.einsum('hqk,qhd->khd', grad_scores, queries)
    grad_proj_in = jnp.concatenate([grad_queries.reshape(row_count, features), grad_keys.reshape(row_count, features), grad_values.reshape(row_count, features)], axis=-1)
    grad_proj_b = grad_proj_in.astype(jnp.bfloat16)
    grad_qkv = matmul(attn_in.T, grad_proj_b)
    grad_attn_in = rounded(matmul(grad_proj_b, qkv_weight.T))
    grad_norm1, gain_one, bias_one = norm_backward(grad_attn_in, hat_one, inv_one, norm1_gain)
    grad_tok = (grad_resid + grad_norm1).astype(jnp.bfloat16)
    terms = (grad_qkv, grad_proj, grad_fc1, grad_fc2, lax.optimization_barrier(jnp.sum(grad_proj_in, axis=0)), grad_proj_bias, lax.optimization_barrier(jnp.sum(grad_pre, axis=0)), gain_one, bias_one, gain_two, bias_two)
    return (tuple((first_term + second_term for first_term, second_term in zip(running, terms))), grad_tok)

def to_windows(field, features):
    rows_x, rows_y, packed = field.shape
    depth_count = packed // features
    shaped = field.reshape(rows_x // WIN, WIN, rows_y // WIN, WIN, depth_count, features)
    return shaped.transpose(0, 2, 1, 3, 4, 5).reshape(-1, WIN * WIN * depth_count, features)

def from_windows(windows, rows_x, rows_y, features):
    depth_count = windows.shape[1] // (WIN * WIN)
    shaped = windows.reshape(rows_x // WIN, rows_y // WIN, WIN, WIN, depth_count, features)
    return shaped.transpose(0, 2, 1, 3, 4, 5).reshape(rows_x, rows_y, depth_count * features)

def reference(tokens, cotangent, qkv_weight, qkv_bias, proj_weight, proj_bias, fc1_weight, fc1_bias, fc2_weight, norm1_gain, norm1_bias, norm2_gain, norm2_bias):
    weights = (qkv_weight, qkv_bias, proj_weight, proj_bias, fc1_weight, fc1_bias, fc2_weight, norm1_gain, norm1_bias, norm2_gain, norm2_bias)
    margin = WIN // 2
    tok_win = to_windows(jnp.roll(tokens, (-margin, -margin), (0, 1)), WIDTH)
    cot_win = to_windows(jnp.roll(cotangent, (-margin, -margin), (0, 1)), WIDTH)
    dims_list = [(WIDTH, 3 * WIDTH), (WIDTH, WIDTH), (WIDTH, MLP_WIDTH), (MLP_WIDTH, WIDTH), (3 * WIDTH,), (WIDTH,), (MLP_WIDTH,), (WIDTH,), (WIDTH,), (WIDTH,), (WIDTH,)]
    initial = tuple((jnp.zeros(dims_shape, jnp.float32) for dims_shape in dims_list))
    running, grad_win = lax.scan(partial(window_pass, weights), initial, (tok_win, cot_win))
    grad_tokens = jnp.roll(from_windows(grad_win, NX, NY, WIDTH), (margin, margin), (0, 1))
    factor = TOKENS ** (-0.5)
    gradients = tuple((entry * factor for entry in running))
    return (grad_tokens, gradients[0], gradients[1], gradients[2], gradients[3], jnp.concatenate(gradients[4:]))
```

```python
from functools import partial

import jax
import jax.numpy as jnp
from jax import lax
from jax.experimental import pallas as pl
from jax.experimental.pallas import tpu as pltpu
from jax.sharding import PartitionSpec as P

HEADS = 6
WIN = 8
LANES = 128
eps = 1e-05
BF16 = jnp.bfloat16
F32 = jnp.float32
BOTH = ("gx", "gy")


def dot_nn(left, right):
    return lax.dot_general(left, right, (((1,), (0,)), ((), ())), preferred_element_type=F32)


def dot_nt(left, right):
    return lax.dot_general(left, right, (((1,), (1,)), ((), ())), preferred_element_type=F32)


def dot_tn(left, right):
    return lax.dot_general(left, right, (((0,), (0,)), ((), ())), preferred_element_type=F32)


def norm_forward(value):
    centred = value - jnp.mean(value, axis=0, keepdims=True)
    inverse = lax.rsqrt(jnp.mean(centred * centred, axis=0, keepdims=True) + eps)
    return centred * inverse, inverse


def norm_backward(incoming, normed, inverse, gain):
    scaled = incoming * gain
    centre = jnp.mean(scaled, axis=0, keepdims=True)
    projection = jnp.mean(scaled * normed, axis=0, keepdims=True)
    return inverse * (scaled - centre - normed * projection)


def token_partial(value):
    total = value[:, :LANES]
    for at in range(LANES, value.shape[1], LANES):
        total = total + value[:, at : at + LANES]
    return total


def gather_window(refs, depth, features):
    field = jnp.concatenate([ref[...] for ref in refs], axis=0)
    return jnp.concatenate(
        [field[:, t * features : (t + 1) * features] for t in range(depth)], axis=0
    )


def window_kernel(
    core, tok0, tok1, tok2, tok3, cot0, cot1, cot2, cot3,
    qkv_wt, qkv_w, proj_wt, proj_w, fc1_wt, fc1_w, fc2_w, columns,
    out0, out1, out2, out3, keep, send,
    attn_ref, gp_ref, grads,
):
    features = proj_w.shape[0]
    hidden_width = fc2_w.shape[0]
    head = features // HEADS
    depth = tok0.shape[1] // features
    scale = head ** (-0.5)
    at = 0
    params = []
    for size in (3 * features, features, hidden_width) + (features,) * 4:
        params.append(columns[at : at + size, 0:1])
        at += size
    qkv_b, proj_b, fc1_b, g1, b1, g2, b2 = params

    tok_t = gather_window((tok0, tok1, tok2, tok3), depth, features).astype(F32).T
    hat1, inv1 = norm_forward(tok_t)
    attn_in = (hat1 * g1 + b1).astype(BF16)
    projected = dot_nn(qkv_wt[...], attn_in) + qkv_b
    queries = (projected[:features] * scale).astype(BF16)
    keys = projected[features : 2 * features].astype(BF16)
    values = projected[2 * features :].astype(BF16)
    blended = []
    for h in range(HEADS):
        rows = slice(h * head, (h + 1) * head)
        scores = dot_tn(keys[rows], queries[rows])
        top = jnp.max(scores, axis=0, keepdims=True)
        raised = jnp.exp(scores - top)
        attention = raised * (1.0 / jnp.sum(raised, axis=0, keepdims=True))
        attn_ref[h] = attention
        blended.append(dot_nn(values[rows], attention.astype(BF16)))
    blended = jnp.concatenate(blended, axis=0).astype(BF16)
    branch = (dot_nn(proj_wt[...], blended) + proj_b).astype(BF16)
    residual = tok_t + branch.astype(F32)
    hat2, inv2 = norm_forward(residual)
    mlp_in = (hat2 * g2 + b2).astype(BF16)

    cot = gather_window((cot0, cot1, cot2, cot3), depth, features)
    cot_t = cot.astype(F32).T
    hidden = dot_nn(fc1_wt[...], mlp_in) + fc1_b
    cdf = 0.5 * (1.0 + lax.erf(hidden * 0.7071067811865476))
    pdf = jnp.exp(-0.5 * hidden * hidden) * 0.3989422804014327
    active = (hidden * cdf).astype(BF16)
    fc2_sum = dot_nn(active, cot).astype(BF16)
    grad_pre = dot_nn(fc2_w[...], cot_t.astype(BF16)) * (cdf + hidden * pdf)
    grad_pre_b = grad_pre.astype(BF16)
    fc1_sum = dot_nt(mlp_in, grad_pre_b).astype(BF16)
    at = 0
    for col in range(0, hidden_width, LANES):
        grads[at : at + features, :] = fc1_sum[:, col : col + LANES]
        at += features
    grads[at : at + hidden_width, :] = fc2_sum[:, :LANES]
    at += hidden_width
    half = hidden_width // 2
    grads[at : at + half, :] = jnp.concatenate(
        [fc2_sum[:half, LANES:], fc2_sum[half:, LANES:]], axis=1
    )
    at += half
    grad_mlp_in = dot_nn(fc1_w[...], grad_pre_b)
    grad_resid = cot_t + norm_backward(grad_mlp_in, hat2, inv2, g2)
    grad_branch = grad_resid.astype(BF16)
    proj_sum = dot_nt(blended, grad_branch).astype(BF16)
    grad_blend = dot_nn(proj_w[...], grad_branch).astype(BF16)

    for h in range(HEADS):
        rows = slice(h * head, (h + 1) * head)
        grad_out = grad_blend[rows]
        attention = attn_ref[h]
        grad_attention = dot_tn(values[rows], grad_out)
        total = jnp.sum(grad_attention * attention, axis=0, keepdims=True)
        grad_scores = (attention * (grad_attention - total)).astype(BF16)
        low = h * head
        gp_ref[low : low + head, :] = dot_nn(keys[rows], grad_scores) * scale
        low += features
        gp_ref[low : low + head, :] = dot_nt(queries[rows], grad_scores)
        low += features
        gp_ref[low : low + head, :] = dot_nt(grad_out, attention.astype(BF16))
    grad_proj_in = gp_ref[...]
    grad_proj_b = grad_proj_in.astype(BF16)
    qkv_sum = dot_nt(attn_in, grad_proj_b).astype(BF16)
    both_sums = jnp.concatenate([qkv_sum, proj_sum], axis=1)
    for col in range(0, 4 * features, LANES):
        grads[at : at + features, :] = both_sums[:, col : col + LANES]
        at += features
    grad_attn_in = dot_nn(qkv_w[...], grad_proj_b).astype(BF16).astype(F32)
    grad_tok = grad_resid + norm_backward(grad_attn_in, hat1, inv1, g1)

    partials = jnp.concatenate(
        [
            token_partial(value)
            for value in (
                grad_proj_in,
                grad_branch.astype(F32),
                grad_pre,
                grad_attn_in * hat1,
                grad_attn_in,
                grad_mlp_in * hat2,
                grad_mlp_in,
            )
        ],
        axis=0,
    )
    high = partials.astype(BF16)
    low = (partials - high.astype(F32)).astype(BF16)
    split = jnp.concatenate([high, low], axis=1)
    sums = dot_nt(jnp.ones((16, 2 * LANES), BF16), split)
    rows = [sums[0:1, i : i + LANES] for i in range(0, sums.shape[1], LANES)]
    rows.append(jnp.zeros((grads.shape[0] - at - len(rows), LANES), F32))
    grads[at:, :] = jnp.concatenate(rows, axis=0).astype(BF16)
    size = keep.shape[0]

    @pl.when(core[0] == 0)
    def _():
        keep[...] = grads[:size, :]
        send[...] = grads[size:, :]

    @pl.when(core[0] != 0)
    def _():
        keep[...] = grads[size:, :]
        send[...] = grads[:size, :]

    rows_t = grad_tok.T.astype(BF16)
    places = rows_t.shape[0] // depth
    quarter = places // 4
    for k, out in enumerate((out0, out1, out2, out3)):
        out[...] = jnp.concatenate(
            [
                rows_t[t * places + k * quarter : t * places + (k + 1) * quarter]
                for t in range(depth)
            ],
            axis=1,
        )


VMEM = pl.BlockSpec(memory_space=pltpu.VMEM)
SMEM = pl.BlockSpec(memory_space=pltpu.SMEM)
PARAMS = pltpu.CompilerParams(vmem_limit_bytes=48 * 1024 * 1024)


def grad_rows(features, hidden_width):
    vector_rows = (8 * features + hidden_width) // LANES
    used = features * (2 * hidden_width + 4 * features) // LANES + vector_rows
    return -(-used // 512) * 512


def window_call(core, toks, cots, prepared, weights):
    qkv_w, proj_w, fc1_w, fc2_w = weights
    features, hidden_width = fc1_w.shape
    tokens = 4 * toks[0].size // features
    rows = grad_rows(features, hidden_width)
    quad = jax.ShapeDtypeStruct(toks[0].shape, BF16)
    half = jax.ShapeDtypeStruct((rows // 2, LANES), BF16)
    qkv_wt, proj_wt, fc1_wt, columns = prepared
    return pl.pallas_call(
        window_kernel,
        out_shape=[quad] * 4 + [half] * 2,
        in_specs=[SMEM] + [VMEM] * 16,
        out_specs=[VMEM] * 6,
        scratch_shapes=[
            pltpu.VMEM((HEADS, tokens, tokens), F32),
            pltpu.VMEM((qkv_w.shape[1], tokens), F32),
            pltpu.VMEM((rows, LANES), BF16),
        ],
        compiler_params=PARAMS,
        name="window",
    )(core, *toks, *cots, qkv_wt, qkv_w, proj_wt, proj_w, fc1_wt, fc1_w, fc2_w, columns)


def prepare_kernel(qkv_w, proj_w, fc1_w, *refs):
    vectors, (qkv_wt, proj_wt, fc1_wt, columns) = refs[:-4], refs[-4:]
    qkv_wt[...] = qkv_w[...].astype(F32).T.astype(BF16)
    proj_wt[...] = proj_w[...].astype(F32).T.astype(BF16)
    fc1_wt[...] = fc1_w[...].astype(F32).T.astype(BF16)
    row = jnp.concatenate([ref[...] for ref in vectors], axis=1)
    columns[...] = jnp.broadcast_to(row, (8, row.shape[1])).T


def prepare(qkv_w, proj_w, fc1_w, vectors):
    vectors = [v[None, :] for v in vectors]
    count = sum(v.size for v in vectors)
    return pl.pallas_call(
        prepare_kernel,
        out_shape=[jax.ShapeDtypeStruct(w.shape[::-1], BF16) for w in (qkv_w, proj_w, fc1_w)]
        + [jax.ShapeDtypeStruct((count, 8), F32)],
        in_specs=[VMEM] * (3 + len(vectors)),
        out_specs=[VMEM] * 4,
        compiler_params=PARAMS,
        name="prepare",
    )(qkv_w, proj_w, fc1_w, *vectors)


def split_kernel(field_ref, *outs):
    margin = WIN // 2
    field = field_ref[...].astype(F32)
    for out, (low_x, low_y) in zip(outs, ((margin, margin), (0, margin), (margin, 0), (0, 0))):
        out[...] = jnp.concatenate(
            [field[low_x + i, low_y : low_y + margin] for i in range(margin)], axis=0
        ).astype(BF16)


def split_quarters(field):
    quad = jax.ShapeDtypeStruct((WIN * WIN // 4, field.shape[2]), BF16)
    return pl.pallas_call(
        split_kernel,
        out_shape=[quad] * 4,
        in_specs=[VMEM],
        out_specs=[VMEM] * 4,
        compiler_params=PARAMS,
        name="split",
    )(field)


def join_kernel(*refs):
    margin = WIN // 2
    own, part_x, part_y, part_xy = [ref[...].astype(F32) for ref in refs[:4]]
    out = refs[4]
    for i in range(margin):
        rows = slice(i * margin, (i + 1) * margin)
        out[i] = jnp.concatenate([part_xy[rows], part_x[rows]], axis=0).astype(BF16)
        out[margin + i] = jnp.concatenate([part_y[rows], own[rows]], axis=0).astype(BF16)


def join_quarters(parts):
    return pl.pallas_call(
        join_kernel,
        out_shape=jax.ShapeDtypeStruct((WIN, WIN, parts[0].shape[1]), BF16),
        in_specs=[VMEM] * 4,
        out_specs=VMEM,
        compiler_params=PARAMS,
        name="join",
    )(*parts)


def exchange(parts, steps):
    own, part_x, part_y, part_xy = parts
    nx, ny = lax.axis_size("gx"), lax.axis_size("gy")
    ring_x = [(i, (i + steps) % nx) for i in range(nx)]
    ring_y = [(i, (i + steps) % ny) for i in range(ny)]
    both = [
        (i * ny + j, ((i + steps) % nx) * ny + (j + steps) % ny)
        for i in range(nx)
        for j in range(ny)
    ]
    return [
        own,
        lax.ppermute(part_x, "gx", ring_x),
        lax.ppermute(part_y, "gy", ring_y),
        lax.ppermute(part_xy, BOTH, both),
    ]


def swap(value, bit):
    return lax.ppermute(value, BOTH, [(i, i ^ bit) for i in range(256)])


CORE = 16
PLANE = [
    [16 * (4 * y + 2 * xh + core) + 8 * xl + z for y in range(4) for xh in (0, 1) for xl in (0, 1)]
    for core in (0, 1)
    for z in range(8)
]


def sum_everywhere(keep, send):
    mine = keep + swap(send, CORE)
    chunk = mine.shape[0] // 16
    pieces = lax.all_to_all(
        mine.reshape(16, chunk, LANES), BOTH, 0, 0, axis_index_groups=PLANE, tiled=True
    )
    total = jnp.sum(pieces.astype(F32), axis=0).astype(BF16)
    for bit in (1, 2, 4):
        total = total + swap(total, bit)
    spread = jnp.broadcast_to(total[None], (16, chunk, LANES))
    whole = lax.all_to_all(spread, BOTH, 0, 0, axis_index_groups=PLANE, tiled=True)
    whole = whole.reshape(-1, LANES)
    return whole, swap(whole, CORE)


def finish_kernel(core, mine, other, o_qkv, o_proj, o_fc1, o_fc2, o_vec, grads, *, factor):
    size = mine.shape[0]

    @pl.when(core[0] == 0)
    def _():
        grads[:size, :] = mine[...]
        grads[size:, :] = other[...]

    @pl.when(core[0] != 0)
    def _():
        grads[:size, :] = other[...]
        grads[size:, :] = mine[...]

    features, hidden_width = o_fc1.shape
    at = 0

    def take(rows):
        nonlocal at
        at += rows
        return grads[at - rows : at, :].astype(F32) * factor

    for col in range(0, hidden_width, LANES):
        o_fc1[:, col : col + LANES] = take(features)
    o_fc2[:, :LANES] = take(hidden_width)
    half = hidden_width // 2
    rest = take(half)
    o_fc2[:half, LANES:] = rest[:, : features - LANES]
    o_fc2[half:, LANES:] = rest[:, features - LANES :]
    both = jnp.concatenate([take(features) for _ in range(4 * features // LANES)], axis=1)
    o_qkv[...] = both[:, : 3 * features]
    o_proj[...] = both[:, 3 * features :]
    o_vec[...] = take(LANES)[: o_vec.shape[0]]


def finish(core, mine, other, shapes, factor):
    rows = shapes[4] // LANES
    outs = [jax.ShapeDtypeStruct(shape, F32) for shape in (*shapes[:4], (rows, LANES))]
    return pl.pallas_call(
        partial(finish_kernel, factor=factor),
        out_shape=outs,
        in_specs=[SMEM, VMEM, VMEM],
        out_specs=[VMEM] * 5,
        scratch_shapes=[pltpu.VMEM((2 * mine.shape[0], LANES), BF16)],
        compiler_params=PARAMS,
        name="finish",
    )(core, mine, other)


def on_device(
    tokens, cotangent, qkv_w, qkv_b, proj_w, proj_b, fc1_w, fc1_b, fc2_w, g1, b1, g2, b2
):
    features = g1.shape[0]
    token_count = tokens.size // features * lax.axis_size("gx") * lax.axis_size("gy")
    factor = float(token_count) ** (-0.5)
    core = (lax.axis_index("gx") % 2).astype(jnp.int32).reshape(1)
    vectors = (qkv_b, proj_b, fc1_b, g1, b1, g2, b2)
    toks = exchange(split_quarters(tokens), -1)
    cots = exchange(split_quarters(cotangent), -1)
    prepared = prepare(qkv_w, proj_w, fc1_w, vectors)
    *quads, keep, send = window_call(core, toks, cots, prepared, (qkv_w, proj_w, fc1_w, fc2_w))
    grad_tokens = join_quarters(exchange(quads, 1))
    mine, other = sum_everywhere(keep, send)
    shapes = [w.shape for w in (qkv_w, proj_w, fc1_w, fc2_w)] + [sum(v.size for v in vectors)]
    grads = finish(core, mine, other, shapes, factor)
    return (grad_tokens, *grads[:4], grads[4].reshape(-1))


def solution(mesh):
    spec = P("gx", "gy", None)
    return jax.shard_map(
        on_device,
        mesh=mesh,
        in_specs=(spec, spec) + (P(),) * 11,
        out_specs=(spec,) + (P(),) * 5,
        check_vma=False,
    )
```

```python
from functools import partial

import jax
import jax.numpy as jnp
from jax import lax
from jax.experimental import pallas as pl
from jax.experimental.pallas import tpu as pltpu
from jax.sharding import PartitionSpec as P

HEADS = 6
WIN = 8
LANES = 128
eps = 1e-05
BF16 = jnp.bfloat16
F32 = jnp.float32
BOTH = ("gx", "gy")


def dot_nn(left, right):
    return lax.dot_general(left, right, (((1,), (0,)), ((), ())), preferred_element_type=F32)


def dot_nt(left, right):
    return lax.dot_general(left, right, (((1,), (1,)), ((), ())), preferred_element_type=F32)


def dot_tn(left, right):
    return lax.dot_general(left, right, (((0,), (0,)), ((), ())), preferred_element_type=F32)


def norm_forward(value):
    centred = value - jnp.mean(value, axis=0, keepdims=True)
    inverse = lax.rsqrt(jnp.mean(centred * centred, axis=0, keepdims=True) + eps)
    return centred * inverse, inverse


def norm_backward(incoming, normed, inverse, gain):
    scaled = incoming * gain
    centre = jnp.mean(scaled, axis=0, keepdims=True)
    projection = jnp.mean(scaled * normed, axis=0, keepdims=True)
    return inverse * (scaled - centre - normed * projection)


def token_partial(value):
    total = value[:, :LANES]
    for at in range(LANES, value.shape[1], LANES):
        total = total + value[:, at : at + LANES]
    return total


def gather_window(refs, which, depth, features):
    rows = refs[0].shape[0] // 2
    field = jnp.concatenate([ref[which * rows : (which + 1) * rows, :] for ref in refs], axis=0)
    return jnp.concatenate(
        [field[:, t * features : (t + 1) * features] for t in range(depth)], axis=0
    )


def window_kernel(
    core, quad0, quad1, quad2, quad3, weights, vectors,
    out0, out1, out2, out3, keep, send,
    attn_ref, gp_ref, grads,
):
    features = weights.shape[0]
    hidden_width = vectors.shape[0] * LANES - 8 * features
    head = features // HEADS
    depth = quad0.shape[1] // features
    quads = (quad0, quad1, quad2, quad3)
    scale = head ** (-0.5)
    at = 0
    fc1_w, fc2_wt, qkv_w, proj_w = [
        weights[:, low : low + size] for low, size in weight_places(features, hidden_width)
    ]
    row = jnp.concatenate([vectors[i : i + 1, :] for i in range(vectors.shape[0])], axis=1)
    columns = jnp.broadcast_to(row, (8, row.shape[1])).T
    params = []
    for size in (3 * features, features, hidden_width) + (features,) * 4:
        params.append(columns[at : at + size, 0:1])
        at += size
    qkv_b, proj_b, fc1_b, g1, b1, g2, b2 = params

    tok_t = gather_window(quads, 0, depth, features).astype(F32).T
    hat1, inv1 = norm_forward(tok_t)
    attn_in = (hat1 * g1 + b1).astype(BF16)
    projected = dot_tn(qkv_w, attn_in) + qkv_b
    queries = (projected[:features] * scale).astype(BF16)
    keys = projected[features : 2 * features].astype(BF16)
    values = projected[2 * features :].astype(BF16)
    blended = []
    for h in range(HEADS):
        rows = slice(h * head, (h + 1) * head)
        scores = dot_tn(keys[rows], queries[rows])
        top = jnp.max(scores, axis=0, keepdims=True)
        raised = jnp.exp(scores - top)
        attention = raised * (1.0 / jnp.sum(raised, axis=0, keepdims=True))
        attn_ref[h] = attention
        blended.append(dot_nn(values[rows], attention.astype(BF16)))
    blended = jnp.concatenate(blended, axis=0).astype(BF16)
    branch = (dot_tn(proj_w, blended) + proj_b).astype(BF16)
    residual = tok_t + branch.astype(F32)
    hat2, inv2 = norm_forward(residual)
    mlp_in = (hat2 * g2 + b2).astype(BF16)

    cot_t = gather_window(quads, 1, depth, features).astype(F32).T
    cot_b = cot_t.astype(BF16)
    hidden = dot_tn(fc1_w, mlp_in) + fc1_b
    cdf = 0.5 * (1.0 + lax.erf(hidden * 0.7071067811865476))
    pdf = jnp.exp(-0.5 * hidden * hidden) * 0.3989422804014327
    active = (hidden * cdf).astype(BF16)
    fc2_sum = dot_nt(cot_b, active).astype(BF16)
    grad_pre = dot_tn(fc2_wt, cot_b) * (cdf + hidden * pdf)
    grad_pre_b = grad_pre.astype(BF16)
    fc1_sum = dot_nt(mlp_in, grad_pre_b).astype(BF16)
    at = 0
    for value in (fc1_sum, fc2_sum):
        for col in range(0, hidden_width, LANES):
            grads[at : at + features, :] = value[:, col : col + LANES]
            at += features
    grad_mlp_in = dot_nn(fc1_w, grad_pre_b)
    grad_resid = cot_t + norm_backward(grad_mlp_in, hat2, inv2, g2)
    grad_branch = grad_resid.astype(BF16)
    proj_sum = dot_nt(blended, grad_branch).astype(BF16)
    grad_blend = dot_nn(proj_w, grad_branch).astype(BF16)

    for h in range(HEADS):
        rows = slice(h * head, (h + 1) * head)
        grad_out = grad_blend[rows]
        attention = attn_ref[h]
        grad_attention = dot_tn(values[rows], grad_out)
        total = jnp.sum(grad_attention * attention, axis=0, keepdims=True)
        grad_scores = (attention * (grad_attention - total)).astype(BF16)
        low = h * head
        gp_ref[low : low + head, :] = dot_nn(keys[rows], grad_scores) * scale
        low += features
        gp_ref[low : low + head, :] = dot_nt(queries[rows], grad_scores)
        low += features
        gp_ref[low : low + head, :] = dot_nt(grad_out, attention.astype(BF16))
    grad_proj_in = gp_ref[...]
    grad_proj_b = grad_proj_in.astype(BF16)
    qkv_sum = dot_nt(attn_in, grad_proj_b).astype(BF16)
    both_sums = jnp.concatenate([qkv_sum, proj_sum], axis=1)
    for col in range(0, 4 * features, LANES):
        grads[at : at + features, :] = both_sums[:, col : col + LANES]
        at += features
    grad_attn_in = dot_nn(qkv_w, grad_proj_b).astype(BF16).astype(F32)
    grad_tok = grad_resid + norm_backward(grad_attn_in, hat1, inv1, g1)

    partials = jnp.concatenate(
        [
            token_partial(value)
            for value in (
                grad_proj_in,
                grad_branch.astype(F32),
                grad_pre,
                grad_attn_in * hat1,
                grad_attn_in,
                grad_mlp_in * hat2,
                grad_mlp_in,
            )
        ],
        axis=0,
    )
    high = partials.astype(BF16)
    low = (partials - high.astype(F32)).astype(BF16)
    split = jnp.concatenate([high, low], axis=1)
    sums = dot_nt(jnp.ones((16, 2 * LANES), BF16), split)
    rows = [sums[0:1, i : i + LANES] for i in range(0, sums.shape[1], LANES)]
    rows.append(jnp.zeros((grads.shape[0] - at - len(rows), LANES), F32))
    grads[at:, :] = jnp.concatenate(rows, axis=0).astype(BF16)
    size = keep.shape[0]

    @pl.when(core[0] == 0)
    def _():
        keep[...] = grads[:size, :]
        send[...] = grads[size:, :]

    @pl.when(core[0] != 0)
    def _():
        keep[...] = grads[size:, :]
        send[...] = grads[:size, :]

    rows_t = grad_tok.T.astype(BF16)
    places = rows_t.shape[0] // depth
    quarter = places // 4
    for k, out in enumerate((out0, out1, out2, out3)):
        out[...] = jnp.concatenate(
            [
                rows_t[t * places + k * quarter : t * places + (k + 1) * quarter]
                for t in range(depth)
            ],
            axis=1,
        )


VMEM = pl.BlockSpec(memory_space=pltpu.VMEM)
SMEM = pl.BlockSpec(memory_space=pltpu.SMEM)
PARAMS = pltpu.CompilerParams(vmem_limit_bytes=48 * 1024 * 1024)


def grad_rows(features, hidden_width):
    vector_rows = (8 * features + hidden_width) // LANES
    used = features * (2 * hidden_width + 4 * features) // LANES + vector_rows
    return -(-used // 512) * 512


def weight_places(features, hidden_width):
    qkv_at = 2 * hidden_width
    proj_at = -(-(qkv_at + 3 * features) // LANES) * LANES
    return (
        (0, hidden_width),
        (hidden_width, hidden_width),
        (qkv_at, 3 * features),
        (proj_at, features),
    )


def window_call(core, quads, weights, vectors):
    features, hidden_width = weights[0].shape
    tokens = 2 * quads[0].size // features
    rows = grad_rows(features, hidden_width)
    places = weight_places(features, hidden_width)
    gap = jnp.zeros((features, places[3][0] - places[2][0] - places[2][1]), BF16)
    joined = jnp.concatenate([*weights[:3], gap, weights[3]], axis=1)
    rows_of_vectors = jnp.concatenate(vectors).reshape(-1, LANES)
    quad = jax.ShapeDtypeStruct((quads[0].shape[0] // 2, quads[0].shape[1]), BF16)
    half = jax.ShapeDtypeStruct((rows // 2, LANES), BF16)
    return pl.pallas_call(
        window_kernel,
        out_shape=[quad] * 4 + [half] * 2,
        in_specs=[SMEM] + [VMEM] * 6,
        out_specs=[VMEM] * 6,
        scratch_shapes=[
            pltpu.VMEM((HEADS, tokens, tokens), F32),
            pltpu.VMEM((3 * features, tokens), F32),
            pltpu.VMEM((rows, LANES), BF16),
        ],
        compiler_params=PARAMS,
        name="window",
    )(core, *quads, joined, rows_of_vectors)


def split_kernel(fields_ref, *outs):
    margin = WIN // 2
    fields = [fields_ref[i].astype(F32) for i in range(2)]
    for out, (low_x, low_y) in zip(outs, ((margin, margin), (0, margin), (margin, 0), (0, 0))):
        out[...] = jnp.concatenate(
            [f[low_x + i, low_y : low_y + margin] for f in fields for i in range(margin)], axis=0
        ).astype(BF16)


def split_quarters(tokens, cotangent):
    quad = jax.ShapeDtypeStruct((WIN * WIN // 2, tokens.shape[2]), BF16)
    return pl.pallas_call(
        split_kernel,
        out_shape=[quad] * 4,
        in_specs=[VMEM],
        out_specs=[VMEM] * 4,
        compiler_params=PARAMS,
        name="split",
    )(jnp.stack([tokens, cotangent]))


def join_kernel(*refs):
    margin = WIN // 2
    own, part_x, part_y, part_xy = [ref[...].astype(F32) for ref in refs[:4]]
    out = refs[4]
    for i in range(margin):
        rows = slice(i * margin, (i + 1) * margin)
        out[i] = jnp.concatenate([part_xy[rows], part_x[rows]], axis=0).astype(BF16)
        out[margin + i] = jnp.concatenate([part_y[rows], own[rows]], axis=0).astype(BF16)


def join_quarters(parts):
    return pl.pallas_call(
        join_kernel,
        out_shape=jax.ShapeDtypeStruct((WIN, WIN, parts[0].shape[1]), BF16),
        in_specs=[VMEM] * 4,
        out_specs=VMEM,
        compiler_params=PARAMS,
        name="join",
    )(*parts)


def exchange(steps):
    nx, ny = lax.axis_size("gx"), lax.axis_size("gy")
    ring_x = [(i, (i + steps) % nx) for i in range(nx)]
    ring_y = [(i, (i + steps) % ny) for i in range(ny)]
    both = [
        (i * ny + j, ((i + steps) % nx) * ny + (j + steps) % ny)
        for i in range(nx)
        for j in range(ny)
    ]
    return (
        lambda value: lax.ppermute(value, "gx", ring_x),
        lambda value: lax.ppermute(value, "gy", ring_y),
        lambda value: lax.ppermute(value, BOTH, both),
    )


def swap(value, bit):
    return lax.ppermute(value, BOTH, [(i, i ^ bit) for i in range(256)])


CORE = 16
PLANE = [
    [16 * (4 * y + 2 * xh + core) + 8 * xl + z for y in range(4) for xh in (0, 1) for xl in (0, 1)]
    for core in (0, 1)
    for z in range(8)
]


def sum_everywhere(keep, send, own, sends):
    mine = keep + swap(send, CORE)
    chunk = mine.shape[0] // 16
    pieces = lax.all_to_all(
        mine.reshape(16, chunk, LANES), BOTH, 0, 0, axis_index_groups=PLANE, tiled=True
    )
    received = [move(value) for value, move in zip(sends, exchange(1))]
    received, pieces = lax.optimization_barrier((received, pieces))
    grad_tokens = join_quarters([own, *received])
    total = jnp.sum(pieces.astype(F32), axis=0).astype(BF16)
    for bit in (1, 2, 7):
        total = total + swap(total, bit)
    grad_tokens, total = lax.optimization_barrier((grad_tokens, total))
    spread = jnp.broadcast_to(total[None], (16, chunk, LANES))
    whole = lax.all_to_all(spread, BOTH, 0, 0, axis_index_groups=PLANE, tiled=True)
    whole = whole.reshape(-1, LANES)
    return whole, swap(whole, CORE), grad_tokens


def finish_kernel(core, mine, other, o_qkv, o_proj, o_fc1, o_fc2, o_vec, grads, *, factor):
    size = mine.shape[0]

    @pl.when(core[0] == 0)
    def _():
        grads[:size, :] = mine[...]
        grads[size:, :] = other[...]

    @pl.when(core[0] != 0)
    def _():
        grads[:size, :] = other[...]
        grads[size:, :] = mine[...]

    features, hidden_width = o_fc1.shape
    at = 0

    def take(rows):
        nonlocal at
        at += rows
        return grads[at - rows : at, :].astype(F32) * factor

    for col in range(0, hidden_width, LANES):
        o_fc1[:, col : col + LANES] = take(features)
    for col in range(0, hidden_width, LANES):
        o_fc2[:, col : col + LANES] = take(features)
    both = jnp.concatenate([take(features) for _ in range(4 * features // LANES)], axis=1)
    o_qkv[...] = both[:, : 3 * features]
    o_proj[...] = both[:, 3 * features :]
    o_vec[...] = take(LANES)[: o_vec.shape[0]]


def finish(core, mine, other, shapes, factor):
    shapes = (*shapes[:3], shapes[3][::-1], (shapes[4] // LANES, LANES))
    outs = [jax.ShapeDtypeStruct(shape, F32) for shape in shapes]
    return pl.pallas_call(
        partial(finish_kernel, factor=factor),
        out_shape=outs,
        in_specs=[SMEM, VMEM, VMEM],
        out_specs=[VMEM] * 5,
        scratch_shapes=[pltpu.VMEM((2 * mine.shape[0], LANES), BF16)],
        compiler_params=PARAMS,
        name="finish",
    )(core, mine, other)


def on_device(
    tokens, cotangent, qkv_w, qkv_b, proj_w, proj_b, fc1_w, fc1_b, fc2_w, g1, b1, g2, b2
):
    features = g1.shape[0]
    token_count = tokens.size // features * lax.axis_size("gx") * lax.axis_size("gy")
    factor = float(token_count) ** (-0.5)
    core = (lax.axis_index("gx") % 2).astype(jnp.int32).reshape(1)
    vectors = (qkv_b, proj_b, fc1_b, g1, b1, g2, b2)
    own, *sends = split_quarters(tokens, cotangent)
    quads = [own] + [move(value) for value, move in zip(sends, exchange(-1))]
    own, *sends, keep, send = window_call(
        core, quads, (fc1_w, fc2_w.T, qkv_w, proj_w), vectors
    )
    mine, other, grad_tokens = sum_everywhere(keep, send, own, sends)
    shapes = [w.shape for w in (qkv_w, proj_w, fc1_w, fc2_w)] + [sum(v.size for v in vectors)]
    grads = finish(core, mine, other, shapes, factor)
    return (grad_tokens, *grads[:3], grads[3].T, grads[4].reshape(-1))


def solution(mesh):
    spec = P("gx", "gy", None)
    return jax.shard_map(
        on_device,
        mesh=mesh,
        in_specs=(spec, spec) + (P(),) * 11,
        out_specs=(spec,) + (P(),) * 5,
        check_vma=False,
    )
```

```python
from functools import partial

import jax
import jax.numpy as jnp
from jax import lax
from jax.experimental import pallas as pl
from jax.experimental.pallas import tpu as pltpu
from jax.sharding import PartitionSpec as P

HEADS = 6
WIN = 8
LANES = 128
eps = 1e-05
BF16 = jnp.bfloat16
F32 = jnp.float32
BOTH = ("gx", "gy")


def dot_nn(left, right):
    return lax.dot_general(left, right, (((1,), (0,)), ((), ())), preferred_element_type=F32)


def dot_nt(left, right):
    return lax.dot_general(left, right, (((1,), (1,)), ((), ())), preferred_element_type=F32)


def dot_tn(left, right):
    return lax.dot_general(left, right, (((0,), (0,)), ((), ())), preferred_element_type=F32)


def norm_forward(value):
    centred = value - jnp.mean(value, axis=0, keepdims=True)
    inverse = lax.rsqrt(jnp.mean(centred * centred, axis=0, keepdims=True) + eps)
    return centred * inverse, inverse


def norm_backward(incoming, normed, inverse, gain):
    scaled = incoming * gain
    centre = jnp.mean(scaled, axis=0, keepdims=True)
    projection = jnp.mean(scaled * normed, axis=0, keepdims=True)
    return inverse * (scaled - centre - normed * projection)


def token_partial(value):
    total = value[:, :LANES]
    for at in range(LANES, value.shape[1], LANES):
        total = total + value[:, at : at + LANES]
    return total


def gather_window(refs, which, depth, features):
    rows = refs[0].shape[0] // 2
    field = jnp.concatenate([ref[which * rows : (which + 1) * rows, :] for ref in refs], axis=0)
    return jnp.concatenate(
        [field[:, t * features : (t + 1) * features] for t in range(depth)], axis=0
    )


def window_kernel(
    core, quad0, quad1, quad2, quad3, weights, turned, columns,
    out0, out1, out2, out3, keep, send,
    attn_ref, score_ref, gp_ref, grads,
):
    features = weights.shape[0]
    hidden_width = columns.shape[0] - 8 * features
    head = features // HEADS
    depth = quad0.shape[1] // features
    quads = (quad0, quad1, quad2, quad3)
    scale = head ** (-0.5)
    at = 0
    places = weight_places(features, hidden_width)
    fc1_w, _, qkv_w, proj_w = [weights[:, low : low + size] for low, size in places]
    fc1_wt, fc2_w, qkv_wt, proj_wt = [turned[low : low + size, :] for low, size in places]
    tokens = depth * WIN * WIN
    params = []
    for size in (3 * features, features, hidden_width) + (features,) * 4:
        params.append(jnp.concatenate([columns[at : at + size, :]] * (tokens // LANES), axis=1))
        at += size
    qkv_b, proj_b, fc1_b, g1, b1, g2, b2 = params

    tok_t = gather_window(quads, 0, depth, features).astype(F32).T
    hat1, inv1 = norm_forward(tok_t)
    attn_in = (hat1 * g1 + b1).astype(BF16)
    projected = dot_nn(qkv_wt, attn_in) + qkv_b
    queries = (projected[:features] * scale).astype(BF16)
    keys = projected[features : 2 * features].astype(BF16)
    values = projected[2 * features :].astype(BF16)
    ones = jnp.ones((16, values.shape[1]), BF16)
    blends, inverses = [], []
    for h in range(HEADS):
        rows = slice(h * head, (h + 1) * head)
        scores = dot_tn(keys[rows], queries[rows])
        attn_ref[h] = jnp.exp(scores - jnp.max(scores, axis=0, keepdims=True)).astype(BF16)
    for h in range(HEADS):
        rows = slice(h * head, (h + 1) * head)
        mixed = dot_nn(jnp.concatenate([values[rows], ones], axis=0), attn_ref[h])
        inverses.append(1.0 / mixed[head : head + 1])
        blends.append(mixed[:head] * inverses[h])
    blended = jnp.concatenate(blends, axis=0).astype(BF16)
    branch = (dot_nn(proj_wt, blended) + proj_b).astype(BF16)
    residual = tok_t + branch.astype(F32)
    hat2, inv2 = norm_forward(residual)
    mlp_in = (hat2 * g2 + b2).astype(BF16)

    cot_t = gather_window(quads, 1, depth, features).astype(F32).T
    cot_b = cot_t.astype(BF16)
    hidden = dot_nn(fc1_wt, mlp_in) + fc1_b
    cdf = 0.5 * (1.0 + lax.erf(hidden * 0.7071067811865476))
    pdf = jnp.exp(-0.5 * hidden * hidden) * 0.3989422804014327
    active = (hidden * cdf).astype(BF16)
    fc2_sum = dot_nt(cot_b, active).astype(BF16)
    grad_pre = dot_nn(fc2_w, cot_b) * (cdf + hidden * pdf)
    grad_pre_b = grad_pre.astype(BF16)
    fc1_sum = dot_nt(mlp_in, grad_pre_b).astype(BF16)
    at = 0
    for value in (fc1_sum, fc2_sum):
        for col in range(0, hidden_width, LANES):
            grads[at : at + features, :] = value[:, col : col + LANES]
            at += features
    grad_mlp_in = dot_nn(fc1_w, grad_pre_b)
    grad_resid = cot_t + norm_backward(grad_mlp_in, hat2, inv2, g2)
    grad_branch = grad_resid.astype(BF16)
    proj_sum = dot_nt(blended, grad_branch).astype(BF16)
    grad_blend = dot_nn(proj_w, grad_branch).astype(BF16)

    grad_outs = []
    for h in range(HEADS):
        rows = slice(h * head, (h + 1) * head)
        grad_out = (grad_blend[rows].astype(F32) * inverses[h]).astype(BF16)
        grad_outs.append(grad_out)
        low = 2 * features + h * head
        gp_ref[low : low + head, :] = dot_nt(grad_out, attn_ref[h])
        total = jnp.sum(grad_out.astype(F32) * blends[h], axis=0, keepdims=True)
        score_ref[h] = (
            attn_ref[h].astype(F32) * (dot_tn(values[rows], grad_out) - total)
        ).astype(BF16)
    for h in range(HEADS):
        rows = slice(h * head, (h + 1) * head)
        grad_scores = score_ref[h]
        low = h * head
        gp_ref[low : low + head, :] = dot_nn(keys[rows], grad_scores) * scale
        low += features
        gp_ref[low : low + head, :] = dot_nt(queries[rows], grad_scores)
    grad_proj_in = gp_ref[...]
    grad_proj_b = grad_proj_in.astype(BF16)
    qkv_sum = dot_nt(attn_in, grad_proj_b).astype(BF16)
    both_sums = jnp.concatenate([qkv_sum, proj_sum], axis=1)
    for col in range(0, 4 * features, LANES):
        grads[at : at + features, :] = both_sums[:, col : col + LANES]
        at += features
    grad_attn_in = dot_nn(qkv_w, grad_proj_b).astype(BF16).astype(F32)
    grad_tok = grad_resid + norm_backward(grad_attn_in, hat1, inv1, g1)

    partials = jnp.concatenate(
        [
            token_partial(value)
            for value in (
                grad_proj_in,
                grad_branch.astype(F32),
                grad_pre,
                grad_attn_in * hat1,
                grad_attn_in,
                grad_mlp_in * hat2,
                grad_mlp_in,
            )
        ],
        axis=0,
    )
    high = partials.astype(BF16)
    low = (partials - high.astype(F32)).astype(BF16)
    split = jnp.concatenate([high, low], axis=1)
    sums = dot_nt(jnp.ones((16, 2 * LANES), BF16), split)
    rows = [sums[0:1, i : i + LANES] for i in range(0, sums.shape[1], LANES)]
    rows.append(jnp.zeros((grads.shape[0] - at - len(rows), LANES), F32))
    grads[at:, :] = jnp.concatenate(rows, axis=0).astype(BF16)
    size = keep.shape[0]

    @pl.when(core[0] == 0)
    def _():
        keep[...] = grads[:size, :]
        send[...] = grads[size:, :]

    @pl.when(core[0] != 0)
    def _():
        keep[...] = grads[size:, :]
        send[...] = grads[:size, :]

    rows_t = grad_tok.T.astype(BF16)
    places = rows_t.shape[0] // depth
    quarter = places // 4
    for k, out in enumerate((out0, out1, out2, out3)):
        out[...] = jnp.concatenate(
            [
                rows_t[t * places + k * quarter : t * places + (k + 1) * quarter]
                for t in range(depth)
            ],
            axis=1,
        )


VMEM = pl.BlockSpec(memory_space=pltpu.VMEM)
SMEM = pl.BlockSpec(memory_space=pltpu.SMEM)
PARAMS = pltpu.CompilerParams(vmem_limit_bytes=48 * 1024 * 1024)


def grad_rows(features, hidden_width):
    vector_rows = (8 * features + hidden_width) // LANES
    used = features * (2 * hidden_width + 4 * features) // LANES + vector_rows
    return -(-used // 512) * 512


def weight_places(features, hidden_width):
    qkv_at = 2 * hidden_width
    proj_at = -(-(qkv_at + 3 * features) // LANES) * LANES
    return (
        (0, hidden_width),
        (hidden_width, hidden_width),
        (qkv_at, 3 * features),
        (proj_at, features),
    )


def prepare_kernel(weights, vectors, turned, columns):
    turned[...] = weights[...].T
    row = jnp.concatenate([vectors[i : i + 1, :] for i in range(vectors.shape[0])], axis=1)
    columns[...] = jnp.broadcast_to(row, (LANES, row.shape[1])).T


def prepare(weights, vectors):
    features, hidden_width = weights[0].shape
    places = weight_places(features, hidden_width)
    gap = jnp.zeros((features, places[3][0] - places[2][0] - places[2][1]), BF16)
    joined = jnp.concatenate([*weights[:3], gap, weights[3]], axis=1)
    rows_of_vectors = jnp.concatenate(vectors).reshape(-1, LANES)
    turned, columns = pl.pallas_call(
        prepare_kernel,
        out_shape=[
            jax.ShapeDtypeStruct(joined.shape[::-1], BF16),
            jax.ShapeDtypeStruct((rows_of_vectors.size, LANES), F32),
        ],
        in_specs=[VMEM] * 2,
        out_specs=[VMEM] * 2,
        compiler_params=PARAMS,
        name="prepare",
    )(joined, rows_of_vectors)
    return joined, turned, columns


def window_call(core, quads, prepared):
    features = prepared[0].shape[0]
    hidden_width = prepared[2].shape[0] - 8 * features
    tokens = 2 * quads[0].size // features
    rows = grad_rows(features, hidden_width)
    quad = jax.ShapeDtypeStruct((quads[0].shape[0] // 2, quads[0].shape[1]), BF16)
    half = jax.ShapeDtypeStruct((rows // 2, LANES), BF16)
    return pl.pallas_call(
        window_kernel,
        out_shape=[quad] * 4 + [half] * 2,
        in_specs=[SMEM] + [VMEM] * 7,
        out_specs=[VMEM] * 6,
        scratch_shapes=[
            pltpu.VMEM((HEADS, tokens, tokens), BF16),
            pltpu.VMEM((HEADS, tokens, tokens), BF16),
            pltpu.VMEM((3 * features, tokens), F32),
            pltpu.VMEM((rows, LANES), BF16),
        ],
        compiler_params=PARAMS,
        name="window",
    )(core, *quads, *prepared)


def split_kernel(fields_ref, *outs):
    margin = WIN // 2
    fields = [fields_ref[i].astype(F32) for i in range(2)]
    for out, (low_x, low_y) in zip(outs, ((margin, margin), (0, margin), (margin, 0), (0, 0))):
        out[...] = jnp.concatenate(
            [f[low_x + i, low_y : low_y + margin] for f in fields for i in range(margin)], axis=0
        ).astype(BF16)


def split_quarters(tokens, cotangent):
    quad = jax.ShapeDtypeStruct((WIN * WIN // 2, tokens.shape[2]), BF16)
    return pl.pallas_call(
        split_kernel,
        out_shape=[quad] * 4,
        in_specs=[VMEM],
        out_specs=[VMEM] * 4,
        compiler_params=PARAMS,
        name="split",
    )(jnp.stack([tokens, cotangent]))


def join_kernel(*refs):
    margin = WIN // 2
    own, part_x, part_y, part_xy = [ref[...].astype(F32) for ref in refs[:4]]
    out = refs[4]
    for i in range(margin):
        rows = slice(i * margin, (i + 1) * margin)
        out[i] = jnp.concatenate([part_xy[rows], part_x[rows]], axis=0).astype(BF16)
        out[margin + i] = jnp.concatenate([part_y[rows], own[rows]], axis=0).astype(BF16)


def join_quarters(parts):
    return pl.pallas_call(
        join_kernel,
        out_shape=jax.ShapeDtypeStruct((WIN, WIN, parts[0].shape[1]), BF16),
        in_specs=[VMEM] * 4,
        out_specs=VMEM,
        compiler_params=PARAMS,
        name="join",
    )(*parts)


def exchange(steps):
    nx, ny = lax.axis_size("gx"), lax.axis_size("gy")
    ring_x = [(i, (i + steps) % nx) for i in range(nx)]
    ring_y = [(i, (i + steps) % ny) for i in range(ny)]
    both = [
        (i * ny + j, ((i + steps) % nx) * ny + (j + steps) % ny)
        for i in range(nx)
        for j in range(ny)
    ]
    return (
        lambda value: lax.ppermute(value, "gx", ring_x),
        lambda value: lax.ppermute(value, "gy", ring_y),
        lambda value: lax.ppermute(value, BOTH, both),
    )


def swap(value, bit):
    return lax.ppermute(value, BOTH, [(i, i ^ bit) for i in range(256)])


CORE = 16
PLANE = [
    [16 * (4 * y + 2 * xh + core) + 8 * xl + z for y in range(4) for xh in (0, 1) for xl in (0, 1)]
    for core in (0, 1)
    for z in range(8)
]


def sum_everywhere(keep, send, own, sends):
    mine = keep + swap(send, CORE)
    chunk = mine.shape[0] // 16
    pieces = lax.all_to_all(
        mine.reshape(16, chunk, LANES), BOTH, 0, 0, axis_index_groups=PLANE, tiled=True
    )
    received = [move(value) for value, move in zip(sends, exchange(1))]
    received, pieces = lax.optimization_barrier((received, pieces))
    grad_tokens = join_quarters([own, *received])
    total = jnp.sum(pieces.astype(F32), axis=0).astype(BF16)
    for bit in (1, 2, 7):
        total = total + swap(total, bit)
    grad_tokens, total = lax.optimization_barrier((grad_tokens, total))
    spread = jnp.broadcast_to(total[None], (16, chunk, LANES))
    whole = lax.all_to_all(spread, BOTH, 0, 0, axis_index_groups=PLANE, tiled=True)
    whole = whole.reshape(-1, LANES)
    return whole, swap(whole, CORE), grad_tokens


def finish_kernel(core, mine, other, o_qkv, o_proj, o_fc1, o_fc2, o_vec, grads, *, factor):
    size = mine.shape[0]

    @pl.when(core[0] == 0)
    def _():
        grads[:size, :] = mine[...]
        grads[size:, :] = other[...]

    @pl.when(core[0] != 0)
    def _():
        grads[:size, :] = other[...]
        grads[size:, :] = mine[...]

    features, hidden_width = o_fc1.shape
    at = 0

    def take(rows):
        nonlocal at
        at += rows
        return grads[at - rows : at, :].astype(F32) * factor

    for col in range(0, hidden_width, LANES):
        o_fc1[:, col : col + LANES] = take(features)
    for col in range(0, hidden_width, LANES):
        o_fc2[:, col : col + LANES] = take(features)
    both = jnp.concatenate([take(features) for _ in range(4 * features // LANES)], axis=1)
    o_qkv[...] = both[:, : 3 * features]
    o_proj[...] = both[:, 3 * features :]
    o_vec[...] = take(LANES)[: o_vec.shape[0]]


def finish(core, mine, other, shapes, factor):
    shapes = (*shapes[:3], shapes[3][::-1], (shapes[4] // LANES, LANES))
    outs = [jax.ShapeDtypeStruct(shape, F32) for shape in shapes]
    return pl.pallas_call(
        partial(finish_kernel, factor=factor),
        out_shape=outs,
        in_specs=[SMEM, VMEM, VMEM],
        out_specs=[VMEM] * 5,
        scratch_shapes=[pltpu.VMEM((2 * mine.shape[0], LANES), BF16)],
        compiler_params=PARAMS,
        name="finish",
    )(core, mine, other)


def on_device(
    tokens, cotangent, qkv_w, qkv_b, proj_w, proj_b, fc1_w, fc1_b, fc2_w, g1, b1, g2, b2
):
    features = g1.shape[0]
    token_count = tokens.size // features * lax.axis_size("gx") * lax.axis_size("gy")
    factor = float(token_count) ** (-0.5)
    core = (lax.axis_index("gx") % 2).astype(jnp.int32).reshape(1)
    vectors = (qkv_b, proj_b, fc1_b, g1, b1, g2, b2)
    own, *sends = split_quarters(tokens, cotangent)
    quads = [own] + [move(value) for value, move in zip(sends, exchange(-1))]
    prepared = prepare((fc1_w, fc2_w.T, qkv_w, proj_w), vectors)
    own, *sends, keep, send = window_call(core, quads, prepared)
    mine, other, grad_tokens = sum_everywhere(keep, send, own, sends)
    shapes = [w.shape for w in (qkv_w, proj_w, fc1_w, fc2_w)] + [sum(v.size for v in vectors)]
    grads = finish(core, mine, other, shapes, factor)
    return (grad_tokens, *grads[:3], grads[3].T, grads[4].reshape(-1))


def solution(mesh):
    spec = P("gx", "gy", None)
    return jax.shard_map(
        on_device,
        mesh=mesh,
        in_specs=(spec, spec) + (P(),) * 11,
        out_specs=(spec,) + (P(),) * 5,
        check_vma=False,
    )
```

```python
from functools import partial

import jax
import jax.numpy as jnp
from jax import lax
from jax.experimental import pallas as pl
from jax.experimental.pallas import tpu as pltpu
from jax.sharding import PartitionSpec as P

HEADS = 6
WIN = 8
LANES = 128
eps = 1e-05
BF16 = jnp.bfloat16
F32 = jnp.float32
BOTH = ("gx", "gy")


def dot_nn(left, right):
    return lax.dot_general(left, right, (((1,), (0,)), ((), ())), preferred_element_type=F32)


def dot_nt(left, right):
    return lax.dot_general(left, right, (((1,), (1,)), ((), ())), preferred_element_type=F32)


def dot_tn(left, right):
    return lax.dot_general(left, right, (((0,), (0,)), ((), ())), preferred_element_type=F32)


def norm_forward(value):
    centred = value - jnp.mean(value, axis=0, keepdims=True)
    inverse = lax.rsqrt(jnp.mean(centred * centred, axis=0, keepdims=True) + eps)
    return centred * inverse, inverse


def norm_backward(incoming, normed, inverse, gain):
    scaled = incoming * gain
    centre = jnp.mean(scaled, axis=0, keepdims=True)
    projection = jnp.mean(scaled * normed, axis=0, keepdims=True)
    return inverse * (scaled - centre - normed * projection)


def token_partial(value):
    total = value[:, :LANES]
    for at in range(LANES, value.shape[1], LANES):
        total = total + value[:, at : at + LANES]
    return total


def gather_window(refs, which, depth, features):
    rows = refs[0].shape[0] // 2
    field = jnp.concatenate([ref[which * rows : (which + 1) * rows, :] for ref in refs], axis=0)
    return jnp.concatenate(
        [field[:, t * features : (t + 1) * features] for t in range(depth)], axis=0
    )


def window_kernel(
    core, quad0, quad1, quad2, quad3, weights, turned, columns,
    out0, out_x, out_y, keep, send,
    attn_ref, score_ref, gp_ref, grads,
):
    features = weights.shape[0]
    hidden_width = columns.shape[0] - 8 * features
    head = features // HEADS
    depth = quad0.shape[1] // features
    quads = (quad0, quad1, quad2, quad3)
    scale = head ** (-0.5)
    at = 0
    places = weight_places(features, hidden_width)
    fc1_w, _, qkv_w, proj_w = [weights[:, low : low + size] for low, size in places]
    fc1_wt, fc2_w, qkv_wt, proj_wt = [turned[low : low + size, :] for low, size in places]
    tokens = depth * WIN * WIN
    params = []
    for size in (3 * features, features, hidden_width) + (features,) * 4:
        params.append(jnp.concatenate([columns[at : at + size, :]] * (tokens // LANES), axis=1))
        at += size
    qkv_b, proj_b, fc1_b, g1, b1, g2, b2 = params

    tok_t = gather_window(quads, 0, depth, features).T.astype(F32)
    hat1, inv1 = norm_forward(tok_t)
    attn_in = (hat1 * g1 + b1).astype(BF16)
    projected = dot_nn(qkv_wt, attn_in) + qkv_b
    queries = (projected[:features] * scale).astype(BF16)
    keys = projected[features : 2 * features].astype(BF16)
    values = projected[2 * features :].astype(BF16)
    keys_t = keys.T
    values_t = values.T
    ones = jnp.ones((16, values.shape[1]), BF16)
    blends, inverses = [], []
    for h in range(HEADS):
        rows = slice(h * head, (h + 1) * head)
        scores = dot_nn(keys_t[:, rows], queries[rows])
        attn_ref[h] = jnp.exp(scores - jnp.max(scores, axis=0, keepdims=True)).astype(BF16)
    for h in range(HEADS):
        rows = slice(h * head, (h + 1) * head)
        mixed = dot_nn(jnp.concatenate([values[rows], ones], axis=0), attn_ref[h])
        inverses.append(1.0 / mixed[head : head + 1])
        blends.append(mixed[:head] * inverses[h])
    blended = jnp.concatenate(blends, axis=0).astype(BF16)
    branch = (dot_nn(proj_wt, blended) + proj_b).astype(BF16)
    residual = tok_t + branch.astype(F32)
    hat2, inv2 = norm_forward(residual)
    mlp_in = (hat2 * g2 + b2).astype(BF16)

    cot_b = gather_window(quads, 1, depth, features).T
    cot_t = cot_b.astype(F32)
    hidden = dot_nn(fc1_wt, mlp_in) + fc1_b
    cdf = 0.5 * (1.0 + lax.erf(hidden * 0.7071067811865476))
    pdf = jnp.exp(-0.5 * hidden * hidden) * 0.3989422804014327
    active = (hidden * cdf).astype(BF16)
    fc2_sum = dot_nt(cot_b, active).astype(BF16)
    grad_pre = dot_nn(fc2_w, cot_b) * (cdf + hidden * pdf)
    grad_pre_b = grad_pre.astype(BF16)
    fc1_sum = dot_nt(mlp_in, grad_pre_b).astype(BF16)
    at = 0
    for value in (fc1_sum, fc2_sum):
        for col in range(0, hidden_width, LANES):
            grads[at : at + features, :] = value[:, col : col + LANES]
            at += features
    grad_mlp_in = dot_nn(fc1_w, grad_pre_b)
    grad_resid = cot_t + norm_backward(grad_mlp_in, hat2, inv2, g2)
    grad_branch = grad_resid.astype(BF16)
    proj_sum = dot_nt(blended, grad_branch).astype(BF16)
    grad_blend = dot_nn(proj_w, grad_branch).astype(BF16)

    grad_outs = []
    def finish_head(h):
        rows = slice(h * head, (h + 1) * head)
        grad_scores = score_ref[h]
        low = h * head
        gp_ref[low : low + head, :] = dot_nn(keys[rows], grad_scores) * scale
        low += features
        gp_ref[low : low + head, :] = dot_nt(queries[rows], grad_scores)

    for h in range(HEADS):
        rows = slice(h * head, (h + 1) * head)
        grad_out = (grad_blend[rows].astype(F32) * inverses[h]).astype(BF16)
        grad_outs.append(grad_out)
        low = 2 * features + h * head
        gp_ref[low : low + head, :] = dot_nt(grad_out, attn_ref[h])
        total = jnp.sum(grad_out.astype(F32) * blends[h], axis=0, keepdims=True)
        score_ref[h] = (
            attn_ref[h].astype(F32) * (dot_nn(values_t[:, rows], grad_out) - total)
        ).astype(BF16)
        if h:
            finish_head(h - 1)
    finish_head(HEADS - 1)
    grad_proj_in = gp_ref[...]
    grad_proj_b = grad_proj_in.astype(BF16)
    qkv_sum = dot_nt(attn_in, grad_proj_b).astype(BF16)
    both_sums = jnp.concatenate([qkv_sum, proj_sum], axis=1)
    for col in range(0, 4 * features, LANES):
        grads[at : at + features, :] = both_sums[:, col : col + LANES]
        at += features
    grad_attn_in = dot_nn(qkv_w, grad_proj_b).astype(BF16).astype(F32)
    grad_tok = grad_resid + norm_backward(grad_attn_in, hat1, inv1, g1)

    partials = jnp.concatenate(
        [
            token_partial(value)
            for value in (
                grad_proj_in,
                grad_branch.astype(F32),
                grad_pre,
                grad_attn_in * hat1,
                grad_attn_in,
                grad_mlp_in * hat2,
                grad_mlp_in,
            )
        ],
        axis=0,
    )
    high = partials.astype(BF16)
    low = (partials - high.astype(F32)).astype(BF16)
    split = jnp.concatenate([high, low], axis=1)
    sums = dot_nt(jnp.ones((16, 2 * LANES), BF16), split)
    rows = [sums[0:1, i : i + LANES] for i in range(0, sums.shape[1], LANES)]
    rows.append(jnp.zeros((grads.shape[0] - at - len(rows), LANES), F32))
    grads[at:, :] = jnp.concatenate(rows, axis=0).astype(BF16)
    size = keep.shape[0]

    @pl.when(core[0] == 0)
    def _():
        keep[...] = grads[:size, :]
        send[...] = grads[size:, :]

    @pl.when(core[0] != 0)
    def _():
        keep[...] = grads[size:, :]
        send[...] = grads[:size, :]

    rows_t = grad_tok.astype(BF16).T
    places = rows_t.shape[0] // depth
    quarter = places // 4
    parts = [
        jnp.concatenate(
            [
                rows_t[t * places + k * quarter : t * places + (k + 1) * quarter]
                for t in range(depth)
            ],
            axis=1,
        )
        for k in range(4)
    ]
    out0[...] = parts[0]
    out_x[...] = jnp.concatenate([parts[1], parts[3]], axis=0)
    out_y[...] = parts[2]


VMEM = pl.BlockSpec(memory_space=pltpu.VMEM)
SMEM = pl.BlockSpec(memory_space=pltpu.SMEM)
PARAMS = pltpu.CompilerParams(vmem_limit_bytes=48 * 1024 * 1024)


def grad_rows(features, hidden_width):
    vector_rows = (8 * features + hidden_width) // LANES
    used = features * (2 * hidden_width + 4 * features) // LANES + vector_rows
    return -(-used // 512) * 512


def weight_places(features, hidden_width):
    qkv_at = 2 * hidden_width
    proj_at = -(-(qkv_at + 3 * features) // LANES) * LANES
    return (
        (0, hidden_width),
        (hidden_width, hidden_width),
        (qkv_at, 3 * features),
        (proj_at, features),
    )


def prepare_kernel(weights, vectors, turned, columns):
    turned[...] = weights[...].T
    row = jnp.concatenate([vectors[i : i + 1, :] for i in range(vectors.shape[0])], axis=1)
    columns[...] = jnp.broadcast_to(row, (LANES, row.shape[1])).T


def prepare(weights, vectors):
    features, hidden_width = weights[0].shape
    places = weight_places(features, hidden_width)
    gap = jnp.zeros((features, places[3][0] - places[2][0] - places[2][1]), BF16)
    joined = jnp.concatenate([*weights[:3], gap, weights[3]], axis=1)
    rows_of_vectors = jnp.concatenate(vectors).reshape(-1, LANES)
    turned, columns = pl.pallas_call(
        prepare_kernel,
        out_shape=[
            jax.ShapeDtypeStruct(joined.shape[::-1], BF16),
            jax.ShapeDtypeStruct((rows_of_vectors.size, LANES), F32),
        ],
        in_specs=[VMEM] * 2,
        out_specs=[VMEM] * 2,
        compiler_params=PARAMS,
        name="prepare",
    )(joined, rows_of_vectors)
    return joined, turned, columns


def window_call(core, quads, prepared):
    features = prepared[0].shape[0]
    hidden_width = prepared[2].shape[0] - 8 * features
    tokens = 2 * quads[0].size // features
    rows = grad_rows(features, hidden_width)
    quad = jax.ShapeDtypeStruct((quads[0].shape[0] // 2, quads[0].shape[1]), BF16)
    half = jax.ShapeDtypeStruct((rows // 2, LANES), BF16)
    return pl.pallas_call(
        window_kernel,
        out_shape=[quad, jax.ShapeDtypeStruct(quads[0].shape, BF16), quad] + [half] * 2,
        in_specs=[SMEM] + [VMEM] * 7,
        out_specs=[VMEM] * 5,
        scratch_shapes=[
            pltpu.VMEM((HEADS, tokens, tokens), BF16),
            pltpu.VMEM((HEADS, tokens, tokens), BF16),
            pltpu.VMEM((3 * features, tokens), F32),
            pltpu.VMEM((rows, LANES), BF16),
        ],
        compiler_params=PARAMS,
        name="window",
    )(core, *quads, *prepared)


def split_kernel(fields_ref, *outs):
    margin = WIN // 2
    fields = [fields_ref[i].astype(F32) for i in range(2)]
    for out, (low_x, low_y) in zip(outs, ((margin, margin), (0, margin), (margin, 0), (0, 0))):
        out[...] = jnp.concatenate(
            [f[low_x + i, low_y : low_y + margin] for f in fields for i in range(margin)], axis=0
        ).astype(BF16)


def split_quarters(tokens, cotangent):
    quad = jax.ShapeDtypeStruct((WIN * WIN // 2, tokens.shape[2]), BF16)
    return pl.pallas_call(
        split_kernel,
        out_shape=[quad] * 4,
        in_specs=[VMEM],
        out_specs=[VMEM] * 4,
        compiler_params=PARAMS,
        name="split",
    )(jnp.stack([tokens, cotangent]))


def join_kernel(*refs):
    margin = WIN // 2
    own, from_x, from_y = [ref[...].astype(F32) for ref in refs[:3]]
    out = refs[3]
    part_x = from_x[: margin * margin]
    part_y, part_xy = from_y[: margin * margin], from_y[margin * margin :]
    for i in range(margin):
        rows = slice(i * margin, (i + 1) * margin)
        out[i] = jnp.concatenate([part_xy[rows], part_x[rows]], axis=0).astype(BF16)
        out[margin + i] = jnp.concatenate([part_y[rows], own[rows]], axis=0).astype(BF16)


def join_quarters(parts):
    return pl.pallas_call(
        join_kernel,
        out_shape=jax.ShapeDtypeStruct((WIN, WIN, parts[0].shape[1]), BF16),
        in_specs=[VMEM] * 3,
        out_specs=VMEM,
        compiler_params=PARAMS,
        name="join",
    )(*parts)


def exchange(steps):
    nx, ny = lax.axis_size("gx"), lax.axis_size("gy")
    ring_x = [(i, (i + steps) % nx) for i in range(nx)]
    ring_y = [(i, (i + steps) % ny) for i in range(ny)]
    both = [
        (i * ny + j, ((i + steps) % nx) * ny + (j + steps) % ny)
        for i in range(nx)
        for j in range(ny)
    ]
    return (
        lambda value: lax.ppermute(value, "gx", ring_x),
        lambda value: lax.ppermute(value, "gy", ring_y),
        lambda value: lax.ppermute(value, BOTH, both),
    )


def swap(value, bit):
    return lax.ppermute(value, BOTH, [(i, i ^ bit) for i in range(256)])


CORE = 16
PLANE = [
    [
        16 * (4 * y + 2 * xh + core) + 8 * xl + 2 * z + zl
        for y in range(4)
        for xh in (0, 1)
        for xl in (0, 1)
        for zl in (0, 1)
    ]
    for core in (0, 1)
    for z in range(4)
]


def sum_everywhere(keep, send, own, sends):
    mine = keep + swap(send, CORE)
    chunk = mine.shape[0] // 32
    pieces = lax.all_to_all(
        mine.reshape(32, chunk, LANES), BOTH, 0, 0, axis_index_groups=PLANE, tiled=True
    )
    hop_x, hop_y, _ = exchange(1)
    from_x = hop_x(sends[0])
    from_y = hop_y(jnp.concatenate([sends[1], from_x[own.shape[0] :]], axis=0))
    grad_tokens = join_quarters([own, from_x, from_y])
    total = jnp.sum(pieces.astype(F32), axis=0).astype(BF16)
    for bit in (2, 6):
        total = total + swap(total, bit)
    grad_tokens, total = lax.optimization_barrier((grad_tokens, total))
    spread = jnp.broadcast_to(total[None], (32, chunk, LANES))
    whole = lax.all_to_all(spread, BOTH, 0, 0, axis_index_groups=PLANE, tiled=True)
    whole = whole.reshape(-1, LANES)
    return whole, swap(whole, CORE), grad_tokens


def finish_kernel(core, mine, other, o_qkv, o_proj, o_fc1, o_fc2, o_vec, grads, *, factor):
    size = mine.shape[0]

    @pl.when(core[0] == 0)
    def _():
        grads[:size, :] = mine[...]
        grads[size:, :] = other[...]

    @pl.when(core[0] != 0)
    def _():
        grads[:size, :] = other[...]
        grads[size:, :] = mine[...]

    features, hidden_width = o_fc1.shape
    at = 0

    def take(rows):
        nonlocal at
        at += rows
        return grads[at - rows : at, :].astype(F32) * factor

    for col in range(0, hidden_width, LANES):
        o_fc1[:, col : col + LANES] = take(features)
    for col in range(0, hidden_width, LANES):
        o_fc2[:, col : col + LANES] = take(features)
    both = jnp.concatenate([take(features) for _ in range(4 * features // LANES)], axis=1)
    o_qkv[...] = both[:, : 3 * features]
    o_proj[...] = both[:, 3 * features :]
    o_vec[...] = take(LANES)[: o_vec.shape[0]]


def finish(core, mine, other, shapes, factor):
    shapes = (*shapes[:3], shapes[3][::-1], (shapes[4] // LANES, LANES))
    outs = [jax.ShapeDtypeStruct(shape, F32) for shape in shapes]
    return pl.pallas_call(
        partial(finish_kernel, factor=factor),
        out_shape=outs,
        in_specs=[SMEM, VMEM, VMEM],
        out_specs=[VMEM] * 5,
        scratch_shapes=[pltpu.VMEM((2 * mine.shape[0], LANES), BF16)],
        compiler_params=PARAMS,
        name="finish",
    )(core, mine, other)


def on_device(
    tokens, cotangent, qkv_w, qkv_b, proj_w, proj_b, fc1_w, fc1_b, fc2_w, g1, b1, g2, b2
):
    features = g1.shape[0]
    token_count = tokens.size // features * lax.axis_size("gx") * lax.axis_size("gy")
    factor = float(token_count) ** (-0.5)
    core = (lax.axis_index("gx") % 2).astype(jnp.int32).reshape(1)
    vectors = (qkv_b, proj_b, fc1_b, g1, b1, g2, b2)
    own, *sends = split_quarters(tokens, cotangent)
    quads = [own] + [move(value) for value, move in zip(sends, exchange(-1))]
    prepared = prepare((fc1_w, fc2_w.T, qkv_w, proj_w), vectors)
    own, *sends, keep, send = window_call(core, quads, prepared)
    mine, other, grad_tokens = sum_everywhere(keep, send, own, sends)
    shapes = [w.shape for w in (qkv_w, proj_w, fc1_w, fc2_w)] + [sum(v.size for v in vectors)]
    grads = finish(core, mine, other, shapes, factor)
    return (grad_tokens, *grads[:3], grads[3].T, grads[4].reshape(-1))


def solution(mesh):
    spec = P("gx", "gy", None)
    return jax.shard_map(
        on_device,
        mesh=mesh,
        in_specs=(spec, spec) + (P(),) * 11,
        out_specs=(spec,) + (P(),) * 5,
        check_vma=False,
    )
```

```python
from functools import partial

import jax
import jax.numpy as jnp
from jax import lax
from jax.experimental import pallas as pl
from jax.experimental.pallas import tpu as pltpu
from jax.sharding import PartitionSpec as P

HEADS = 6
WIN = 8
LANES = 128
eps = 1e-05
BF16 = jnp.bfloat16
F32 = jnp.float32
BOTH = ("gx", "gy")


def dot_nn(left, right):
    return lax.dot_general(left, right, (((1,), (0,)), ((), ())), preferred_element_type=F32)


def dot_nt(left, right):
    return lax.dot_general(left, right, (((1,), (1,)), ((), ())), preferred_element_type=F32)


def dot_tn(left, right):
    return lax.dot_general(left, right, (((0,), (0,)), ((), ())), preferred_element_type=F32)


def norm_forward(value):
    centred = value - jnp.mean(value, axis=0, keepdims=True)
    inverse = lax.rsqrt(jnp.mean(centred * centred, axis=0, keepdims=True) + eps)
    return centred * inverse, inverse


def norm_backward(incoming, normed, inverse, gain):
    scaled = incoming * gain
    centre = jnp.mean(scaled, axis=0, keepdims=True)
    projection = jnp.mean(scaled * normed, axis=0, keepdims=True)
    return inverse * (scaled - centre - normed * projection)


def token_partial(value):
    total = value[:, :LANES]
    for at in range(LANES, value.shape[1], LANES):
        total = total + value[:, at : at + LANES]
    return total


def gather_window(refs, which, depth, features):
    rows = refs[0].shape[0] // 2
    field = jnp.concatenate([ref[which * rows : (which + 1) * rows, :] for ref in refs], axis=0)
    return jnp.concatenate(
        [field[:, t * features : (t + 1) * features] for t in range(depth)], axis=0
    )


def window_kernel(
    core, quad0, quad1, quad2, quad3, weights, turned, columns,
    out0, out1, out2, out3, keep, send,
    attn_ref, score_ref, gp_ref, grads,
):
    features = weights.shape[0]
    hidden_width = columns.shape[0] - 8 * features
    head = features // HEADS
    depth = quad0.shape[1] // features
    quads = (quad0, quad1, quad2, quad3)
    scale = head ** (-0.5)
    at = 0
    places = weight_places(features, hidden_width)
    fc1_w, _, qkv_w, proj_w = [weights[:, low : low + size] for low, size in places]
    fc1_wt, fc2_w, qkv_wt, proj_wt = [turned[low : low + size, :] for low, size in places]
    tokens = depth * WIN * WIN
    params = []
    for size in (3 * features, features, hidden_width) + (features,) * 4:
        params.append(jnp.concatenate([columns[at : at + size, :]] * (tokens // LANES), axis=1))
        at += size
    qkv_b, proj_b, fc1_b, g1, b1, g2, b2 = params

    tok_t = gather_window(quads, 0, depth, features).T.astype(F32)
    hat1, inv1 = norm_forward(tok_t)
    attn_in = (hat1 * g1 + b1).astype(BF16)
    projected = dot_nn(qkv_wt, attn_in) + qkv_b
    queries = (projected[:features] * scale).astype(BF16)
    keys = projected[features : 2 * features].astype(BF16)
    values = projected[2 * features :].astype(BF16)
    keys_t = keys.T
    values_t = values.T
    ones = jnp.ones((16, values.shape[1]), BF16)
    blends, inverses = [], []
    for h in range(HEADS):
        rows = slice(h * head, (h + 1) * head)
        scores = dot_nn(keys_t[:, rows], queries[rows])
        attn_ref[h] = jnp.exp(scores - jnp.max(scores, axis=0, keepdims=True)).astype(BF16)
    for h in range(HEADS):
        rows = slice(h * head, (h + 1) * head)
        mixed = dot_nn(jnp.concatenate([values[rows], ones], axis=0), attn_ref[h])
        inverses.append(1.0 / mixed[head : head + 1])
        blends.append(mixed[:head] * inverses[h])
    blended = jnp.concatenate(blends, axis=0).astype(BF16)
    branch = (dot_nn(proj_wt, blended) + proj_b).astype(BF16)
    residual = tok_t + branch.astype(F32)
    hat2, inv2 = norm_forward(residual)
    mlp_in = (hat2 * g2 + b2).astype(BF16)

    cot_b = gather_window(quads, 1, depth, features).T
    cot_t = cot_b.astype(F32)
    hidden = dot_nn(fc1_wt, mlp_in) + fc1_b
    cdf = 0.5 * (1.0 + lax.erf(hidden * 0.7071067811865476))
    pdf = jnp.exp(-0.5 * hidden * hidden) * 0.3989422804014327
    active = (hidden * cdf).astype(BF16)
    fc2_sum = dot_nt(cot_b, active).astype(BF16)
    grad_pre = dot_nn(fc2_w, cot_b) * (cdf + hidden * pdf)
    grad_pre_b = grad_pre.astype(BF16)
    fc1_sum = dot_nt(mlp_in, grad_pre_b).astype(BF16)
    at = 0
    for value in (fc1_sum, fc2_sum):
        for col in range(0, hidden_width, LANES):
            grads[at : at + features, :] = value[:, col : col + LANES]
            at += features
    grad_mlp_in = dot_nn(fc1_w, grad_pre_b)
    grad_resid = cot_t + norm_backward(grad_mlp_in, hat2, inv2, g2)
    grad_branch = grad_resid.astype(BF16)
    proj_sum = dot_nt(blended, grad_branch).astype(BF16)
    grad_blend = dot_nn(proj_w, grad_branch).astype(BF16)

    grad_outs = []
    def finish_head(h):
        rows = slice(h * head, (h + 1) * head)
        grad_scores = score_ref[h]
        low = h * head
        gp_ref[low : low + head, :] = dot_nn(keys[rows], grad_scores) * scale
        low += features
        gp_ref[low : low + head, :] = dot_nt(queries[rows], grad_scores)

    for h in range(HEADS):
        rows = slice(h * head, (h + 1) * head)
        grad_outs.append((grad_blend[rows].astype(F32) * inverses[h]).astype(BF16))
    for h in range(HEADS):
        rows = slice(h * head, (h + 1) * head)
        grad_out = grad_outs[h]
        grad_attention = dot_nn(values_t[:, rows], grad_out)
        if h:
            finish_head(h - 1)
        low = 2 * features + h * head
        gp_ref[low : low + head, :] = dot_nt(grad_out, attn_ref[h])
        total = jnp.sum(grad_out.astype(F32) * blends[h], axis=0, keepdims=True)
        score_ref[h] = (attn_ref[h].astype(F32) * (grad_attention - total)).astype(BF16)
    finish_head(HEADS - 1)
    grad_proj_in = gp_ref[...]
    grad_proj_b = grad_proj_in.astype(BF16)
    qkv_sum = dot_nt(attn_in, grad_proj_b).astype(BF16)
    both_sums = jnp.concatenate([qkv_sum, proj_sum], axis=1)
    for col in range(0, 4 * features, LANES):
        grads[at : at + features, :] = both_sums[:, col : col + LANES]
        at += features
    grad_attn_in = dot_nn(qkv_w, grad_proj_b).astype(BF16).astype(F32)
    grad_tok = grad_resid + norm_backward(grad_attn_in, hat1, inv1, g1)

    partials = jnp.concatenate(
        [
            token_partial(value)
            for value in (
                grad_proj_in,
                grad_branch.astype(F32),
                grad_pre,
                grad_attn_in * hat1,
                grad_attn_in,
                grad_mlp_in * hat2,
                grad_mlp_in,
            )
        ],
        axis=0,
    )
    high = partials.astype(BF16)
    low = (partials - high.astype(F32)).astype(BF16)
    split = jnp.concatenate([high, low], axis=1)
    sums = dot_nt(jnp.ones((16, 2 * LANES), BF16), split)
    rows = [sums[0:1, i : i + LANES] for i in range(0, sums.shape[1], LANES)]
    rows.append(jnp.zeros((grads.shape[0] - at - len(rows), LANES), F32))
    grads[at:, :] = jnp.concatenate(rows, axis=0).astype(BF16)
    size = keep.shape[0]

    @pl.when(core[0] == 0)
    def _():
        keep[...] = grads[:size, :]
        send[...] = grads[size:, :]

    @pl.when(core[0] != 0)
    def _():
        keep[...] = grads[size:, :]
        send[...] = grads[:size, :]

    rows_t = grad_tok.astype(BF16).T
    places = rows_t.shape[0] // depth
    quarter = places // 4
    for k, out in enumerate((out0, out1, out2, out3)):
        out[...] = jnp.concatenate(
            [
                rows_t[t * places + k * quarter : t * places + (k + 1) * quarter]
                for t in range(depth)
            ],
            axis=1,
        )


VMEM = pl.BlockSpec(memory_space=pltpu.VMEM)
SMEM = pl.BlockSpec(memory_space=pltpu.SMEM)
PARAMS = pltpu.CompilerParams(vmem_limit_bytes=48 * 1024 * 1024)


def grad_rows(features, hidden_width):
    vector_rows = (8 * features + hidden_width) // LANES
    used = features * (2 * hidden_width + 4 * features) // LANES + vector_rows
    return -(-used // 512) * 512


def weight_places(features, hidden_width):
    qkv_at = 2 * hidden_width
    proj_at = -(-(qkv_at + 3 * features) // LANES) * LANES
    return (
        (0, hidden_width),
        (hidden_width, hidden_width),
        (qkv_at, 3 * features),
        (proj_at, features),
    )


def prepare_kernel(weights, vectors, turned, columns):
    turned[...] = weights[...].T
    row = jnp.concatenate([vectors[i : i + 1, :] for i in range(vectors.shape[0])], axis=1)
    columns[...] = jnp.broadcast_to(row, (LANES, row.shape[1])).T


def prepare(weights, vectors):
    features, hidden_width = weights[0].shape
    places = weight_places(features, hidden_width)
    gap = jnp.zeros((features, places[3][0] - places[2][0] - places[2][1]), BF16)
    joined = jnp.concatenate([*weights[:3], gap, weights[3]], axis=1)
    rows_of_vectors = jnp.concatenate(vectors).reshape(-1, LANES)
    turned, columns = pl.pallas_call(
        prepare_kernel,
        out_shape=[
            jax.ShapeDtypeStruct(joined.shape[::-1], BF16),
            jax.ShapeDtypeStruct((rows_of_vectors.size, LANES), F32),
        ],
        in_specs=[VMEM] * 2,
        out_specs=[VMEM] * 2,
        compiler_params=PARAMS,
        name="prepare",
    )(joined, rows_of_vectors)
    return joined, turned, columns


def window_call(core, quads, prepared):
    features = prepared[0].shape[0]
    hidden_width = prepared[2].shape[0] - 8 * features
    tokens = 2 * quads[0].size // features
    rows = grad_rows(features, hidden_width)
    quad = jax.ShapeDtypeStruct((quads[0].shape[0] // 2, quads[0].shape[1]), BF16)
    half = jax.ShapeDtypeStruct((rows // 2, LANES), BF16)
    return pl.pallas_call(
        window_kernel,
        out_shape=[quad] * 4 + [half] * 2,
        in_specs=[SMEM] + [VMEM] * 7,
        out_specs=[VMEM] * 6,
        scratch_shapes=[
            pltpu.VMEM((HEADS, tokens, tokens), BF16),
            pltpu.VMEM((HEADS, tokens, tokens), BF16),
            pltpu.VMEM((3 * features, tokens), F32),
            pltpu.VMEM((rows, LANES), BF16),
        ],
        compiler_params=PARAMS,
        name="window",
    )(core, *quads, *prepared)


def split_kernel(fields_ref, *outs):
    margin = WIN // 2
    fields = [fields_ref[i].astype(F32) for i in range(2)]
    for out, (low_x, low_y) in zip(outs, ((margin, margin), (0, margin), (margin, 0), (0, 0))):
        out[...] = jnp.concatenate(
            [f[low_x + i, low_y : low_y + margin] for f in fields for i in range(margin)], axis=0
        ).astype(BF16)


def split_quarters(tokens, cotangent):
    quad = jax.ShapeDtypeStruct((WIN * WIN // 2, tokens.shape[2]), BF16)
    return pl.pallas_call(
        split_kernel,
        out_shape=[quad] * 4,
        in_specs=[VMEM],
        out_specs=[VMEM] * 4,
        compiler_params=PARAMS,
        name="split",
    )(jnp.stack([tokens, cotangent]))


def join_kernel(*refs):
    margin = WIN // 2
    own, part_x, part_y, part_xy = [ref[...].astype(F32) for ref in refs[:4]]
    out = refs[4]
    for i in range(margin):
        rows = slice(i * margin, (i + 1) * margin)
        out[i] = jnp.concatenate([part_xy[rows], part_x[rows]], axis=0).astype(BF16)
        out[margin + i] = jnp.concatenate([part_y[rows], own[rows]], axis=0).astype(BF16)


def join_quarters(parts):
    return pl.pallas_call(
        join_kernel,
        out_shape=jax.ShapeDtypeStruct((WIN, WIN, parts[0].shape[1]), BF16),
        in_specs=[VMEM] * 4,
        out_specs=VMEM,
        compiler_params=PARAMS,
        name="join",
    )(*parts)


def exchange(steps):
    nx, ny = lax.axis_size("gx"), lax.axis_size("gy")
    ring_x = [(i, (i + steps) % nx) for i in range(nx)]
    ring_y = [(i, (i + steps) % ny) for i in range(ny)]
    both = [
        (i * ny + j, ((i + steps) % nx) * ny + (j + steps) % ny)
        for i in range(nx)
        for j in range(ny)
    ]
    return (
        lambda value: lax.ppermute(value, "gx", ring_x),
        lambda value: lax.ppermute(value, "gy", ring_y),
        lambda value: lax.ppermute(value, BOTH, both),
    )


def swap(value, bit):
    return lax.ppermute(value, BOTH, [(i, i ^ bit) for i in range(256)])


CORE = 16
PLANE = [
    [
        16 * (4 * y + 2 * xh + core) + 8 * xl + 2 * z + zl
        for y in range(4)
        for xh in (0, 1)
        for xl in (0, 1)
        for zl in (0, 1)
    ]
    for core in (0, 1)
    for z in range(4)
]


def sum_everywhere(keep, send, own, sends):
    mine = keep + swap(send, CORE)
    chunk = mine.shape[0] // 32
    pieces = lax.all_to_all(
        mine.reshape(32, chunk, LANES), BOTH, 0, 0, axis_index_groups=PLANE, tiled=True
    )
    received = [move(value) for value, move in zip(sends, exchange(1))]
    grad_tokens = join_quarters([own, *received])
    total = jnp.sum(pieces.astype(F32), axis=0).astype(BF16)
    for bit in (2, 6):
        total = total + swap(total, bit)
    grad_tokens, total = lax.optimization_barrier((grad_tokens, total))
    spread = jnp.broadcast_to(total[None], (32, chunk, LANES))
    whole = lax.all_to_all(spread, BOTH, 0, 0, axis_index_groups=PLANE, tiled=True)
    whole = whole.reshape(-1, LANES)
    return whole, swap(whole, CORE), grad_tokens


def finish_kernel(core, mine, other, o_qkv, o_proj, o_fc1, o_fc2, o_vec, *, factor):
    features, hidden_width = o_fc1.shape
    size = mine.shape[0]

    def unpack(first, second):
        at = 0

        def take(rows):
            nonlocal at
            low, at = at, at + rows
            if at <= size:
                value = first[low:at, :]
            elif low >= size:
                value = second[low - size : at - size, :]
            else:
                value = jnp.concatenate([first[low:, :], second[: at - size, :]], axis=0)
            return value.astype(F32) * factor

        for out in (o_fc1, o_fc2):
            for col in range(0, hidden_width, LANES):
                out[:, col : col + LANES] = take(features)
        both = jnp.concatenate([take(features) for _ in range(4 * features // LANES)], axis=1)
        o_qkv[...] = both[:, : 3 * features]
        o_proj[...] = both[:, 3 * features :]
        o_vec[...] = take(LANES)[: o_vec.shape[0]]

    @pl.when(core[0] == 0)
    def _():
        unpack(mine, other)

    @pl.when(core[0] != 0)
    def _():
        unpack(other, mine)


def finish(core, mine, other, shapes, factor):
    shapes = (*shapes[:3], shapes[3][::-1], (shapes[4] // LANES, LANES))
    outs = [jax.ShapeDtypeStruct(shape, F32) for shape in shapes]
    return pl.pallas_call(
        partial(finish_kernel, factor=factor),
        out_shape=outs,
        in_specs=[SMEM, VMEM, VMEM],
        out_specs=[VMEM] * 5,
        compiler_params=PARAMS,
        name="finish",
    )(core, mine, other)


def on_device(
    tokens, cotangent, qkv_w, qkv_b, proj_w, proj_b, fc1_w, fc1_b, fc2_w, g1, b1, g2, b2
):
    features = g1.shape[0]
    token_count = tokens.size // features * lax.axis_size("gx") * lax.axis_size("gy")
    factor = float(token_count) ** (-0.5)
    core = (lax.axis_index("gx") % 2).astype(jnp.int32).reshape(1)
    vectors = (qkv_b, proj_b, fc1_b, g1, b1, g2, b2)
    own, *sends = split_quarters(tokens, cotangent)
    quads = [own] + [move(value) for value, move in zip(sends, exchange(-1))]
    prepared = prepare((fc1_w, fc2_w.T, qkv_w, proj_w), vectors)
    own, *sends, keep, send = window_call(core, quads, prepared)
    mine, other, grad_tokens = sum_everywhere(keep, send, own, sends)
    shapes = [w.shape for w in (qkv_w, proj_w, fc1_w, fc2_w)] + [sum(v.size for v in vectors)]
    grads = finish(core, mine, other, shapes, factor)
    return (grad_tokens, *grads[:3], grads[3].T, grads[4].reshape(-1))


def solution(mesh):
    spec = P("gx", "gy", None)
    return jax.shard_map(
        on_device,
        mesh=mesh,
        in_specs=(spec, spec) + (P(),) * 11,
        out_specs=(spec,) + (P(),) * 5,
        check_vma=False,
    )
```

```python
from functools import partial

import jax
import jax.numpy as jnp
from jax import lax
from jax.experimental import pallas as pl
from jax.experimental.pallas import tpu as pltpu
from jax.sharding import PartitionSpec as P

HEADS = 6
WIN = 8
LANES = 128
eps = 1e-05
BF16 = jnp.bfloat16
F32 = jnp.float32
BOTH = ("gx", "gy")


def dot_nn(left, right):
    return lax.dot_general(left, right, (((1,), (0,)), ((), ())), preferred_element_type=F32)


def dot_nt(left, right):
    return lax.dot_general(left, right, (((1,), (1,)), ((), ())), preferred_element_type=F32)


def dot_tn(left, right):
    return lax.dot_general(left, right, (((0,), (0,)), ((), ())), preferred_element_type=F32)


def norm_forward(value):
    centred = value - jnp.mean(value, axis=0, keepdims=True)
    inverse = lax.rsqrt(jnp.mean(centred * centred, axis=0, keepdims=True) + eps)
    return centred * inverse, inverse


def norm_backward(incoming, normed, inverse, gain):
    scaled = incoming * gain
    centre = jnp.mean(scaled, axis=0, keepdims=True)
    projection = jnp.mean(scaled * normed, axis=0, keepdims=True)
    return inverse * (scaled - centre - normed * projection)


def token_partial(value):
    total = value[:, :LANES]
    for at in range(LANES, value.shape[1], LANES):
        total = total + value[:, at : at + LANES]
    return total


def gather_window(refs, which, depth, features):
    rows = refs[0].shape[0] // 2
    field = jnp.concatenate([ref[which * rows : (which + 1) * rows, :] for ref in refs], axis=0)
    return jnp.concatenate(
        [field[:, t * features : (t + 1) * features] for t in range(depth)], axis=0
    )


def window_kernel(
    core, quad0, quad1, quad2, quad3, weights, turned, columns,
    out0, out1, out2, out3, keep, send,
    attn_ref, score_ref, gp_ref, grads,
):
    features = weights.shape[0]
    hidden_width = columns.shape[0] - 8 * features
    head = features // HEADS
    depth = quad0.shape[1] // features
    quads = (quad0, quad1, quad2, quad3)
    scale = head ** (-0.5)
    at = 0
    places = weight_places(features, hidden_width)
    fc1_w, _, qkv_w, proj_w = [weights[:, low : low + size] for low, size in places]
    fc1_wt, fc2_w, qkv_wt, proj_wt = [turned[low : low + size, :] for low, size in places]
    tokens = depth * WIN * WIN
    params = []
    for size in (3 * features, features, hidden_width) + (features,) * 4:
        params.append(jnp.concatenate([columns[at : at + size, :]] * (tokens // LANES), axis=1))
        at += size
    qkv_b, proj_b, fc1_b, g1, b1, g2, b2 = params

    tok_t = gather_window(quads, 0, depth, features).T.astype(F32)
    hat1, inv1 = norm_forward(tok_t)
    attn_in = (hat1 * g1 + b1).astype(BF16)
    projected = dot_nn(qkv_wt, attn_in) + qkv_b
    queries = (projected[:features] * scale).astype(BF16)
    keys = projected[features : 2 * features].astype(BF16)
    values = projected[2 * features :].astype(BF16)
    keys_t = keys.T
    values_t = values.T
    ones = jnp.ones((16, values.shape[1]), BF16)
    blends, inverses = [], []
    for h in range(HEADS):
        rows = slice(h * head, (h + 1) * head)
        scores = dot_nn(keys_t[:, rows], queries[rows])
        attn_ref[h] = jnp.exp(scores - jnp.max(scores, axis=0, keepdims=True)).astype(BF16)
    for h in range(HEADS):
        rows = slice(h * head, (h + 1) * head)
        mixed = dot_nn(jnp.concatenate([values[rows], ones], axis=0), attn_ref[h])
        inverses.append(1.0 / mixed[head : head + 1])
        blends.append(mixed[:head] * inverses[h])
    blended = jnp.concatenate(blends, axis=0).astype(BF16)
    branch = (dot_nn(proj_wt, blended) + proj_b).astype(BF16)
    residual = tok_t + branch.astype(F32)
    hat2, inv2 = norm_forward(residual)
    mlp_in = (hat2 * g2 + b2).astype(BF16)

    cot_b = gather_window(quads, 1, depth, features).T
    cot_t = cot_b.astype(F32)
    hidden = dot_nn(fc1_wt, mlp_in) + fc1_b
    cdf = 0.5 * (1.0 + lax.erf(hidden * 0.7071067811865476))
    pdf = jnp.exp(-0.5 * hidden * hidden) * 0.3989422804014327
    active = (hidden * cdf).astype(BF16)
    fc2_sum = dot_nt(cot_b, active).astype(BF16)
    grad_pre = dot_nn(fc2_w, cot_b) * (cdf + hidden * pdf)
    grad_pre_b = grad_pre.astype(BF16)
    fc1_sum = dot_nt(mlp_in, grad_pre_b).astype(BF16)
    at = 0
    for value in (fc1_sum, fc2_sum):
        for col in range(0, hidden_width, LANES):
            grads[at : at + features, :] = value[:, col : col + LANES]
            at += features
    grad_mlp_in = dot_nn(fc1_w, grad_pre_b)
    grad_resid = cot_t + norm_backward(grad_mlp_in, hat2, inv2, g2)
    grad_branch = grad_resid.astype(BF16)
    proj_sum = dot_nt(blended, grad_branch).astype(BF16)
    grad_blend = dot_nn(proj_w, grad_branch).astype(BF16)

    grad_outs = []
    def finish_head(h):
        rows = slice(h * head, (h + 1) * head)
        grad_scores = score_ref[h]
        low = h * head
        gp_ref[low : low + head, :] = dot_nn(keys[rows], grad_scores) * scale
        low += features
        gp_ref[low : low + head, :] = dot_nt(queries[rows], grad_scores)

    for h in range(HEADS):
        rows = slice(h * head, (h + 1) * head)
        grad_outs.append((grad_blend[rows].astype(F32) * inverses[h]).astype(BF16))
    for h in range(HEADS):
        rows = slice(h * head, (h + 1) * head)
        grad_out = grad_outs[h]
        grad_attention = dot_nn(values_t[:, rows], grad_out)
        if h:
            finish_head(h - 1)
        low = 2 * features + h * head
        gp_ref[low : low + head, :] = dot_nt(grad_out, attn_ref[h])
        total = jnp.sum(grad_out.astype(F32) * blends[h], axis=0, keepdims=True)
        score_ref[h] = (attn_ref[h].astype(F32) * (grad_attention - total)).astype(BF16)
    finish_head(HEADS - 1)
    grad_proj_in = gp_ref[...]
    grad_proj_b = grad_proj_in.astype(BF16)
    qkv_sum = dot_nt(attn_in, grad_proj_b).astype(BF16)
    both_sums = jnp.concatenate([qkv_sum, proj_sum], axis=1)
    for col in range(0, 4 * features, LANES):
        grads[at : at + features, :] = both_sums[:, col : col + LANES]
        at += features
    grad_attn_in = dot_nn(qkv_w, grad_proj_b).astype(BF16).astype(F32)
    grad_tok = grad_resid + norm_backward(grad_attn_in, hat1, inv1, g1)

    partials = jnp.concatenate(
        [
            token_partial(value)
            for value in (
                grad_proj_in,
                grad_branch.astype(F32),
                grad_pre,
                grad_attn_in * hat1,
                grad_attn_in,
                grad_mlp_in * hat2,
                grad_mlp_in,
            )
        ],
        axis=0,
    )
    high = partials.astype(BF16)
    low = (partials - high.astype(F32)).astype(BF16)
    split = jnp.concatenate([high, low], axis=1)
    sums = dot_nt(jnp.ones((16, 2 * LANES), BF16), split)
    rows = [sums[0:1, i : i + LANES] for i in range(0, sums.shape[1], LANES)]
    rows.append(jnp.zeros((grads.shape[0] - at - len(rows), LANES), F32))
    grads[at:, :] = jnp.concatenate(rows, axis=0).astype(BF16)
    size = keep.shape[0]

    @pl.when(core[0] == 0)
    def _():
        keep[...] = grads[:size, :]
        send[...] = grads[size:, :]

    @pl.when(core[0] != 0)
    def _():
        keep[...] = grads[size:, :]
        send[...] = grads[:size, :]

    rows_t = grad_tok.astype(BF16).T
    places = rows_t.shape[0] // depth
    quarter = places // 4
    for k, out in enumerate((out0, out1, out2, out3)):
        out[...] = jnp.concatenate(
            [
                rows_t[t * places + k * quarter : t * places + (k + 1) * quarter]
                for t in range(depth)
            ],
            axis=1,
        )


VMEM = pl.BlockSpec(memory_space=pltpu.VMEM)
SMEM = pl.BlockSpec(memory_space=pltpu.SMEM)
PARAMS = pltpu.CompilerParams(vmem_limit_bytes=48 * 1024 * 1024)


def grad_rows(features, hidden_width):
    vector_rows = (8 * features + hidden_width) // LANES
    used = features * (2 * hidden_width + 4 * features) // LANES + vector_rows
    return -(-used // 512) * 512


def weight_places(features, hidden_width):
    qkv_at = 2 * hidden_width
    proj_at = -(-(qkv_at + 3 * features) // LANES) * LANES
    return (
        (0, hidden_width),
        (hidden_width, hidden_width),
        (qkv_at, 3 * features),
        (proj_at, features),
    )


def prepare_kernel(weights, vectors, turned, columns):
    turned[...] = weights[...].T
    row = jnp.concatenate([vectors[i : i + 1, :] for i in range(vectors.shape[0])], axis=1)
    columns[...] = jnp.broadcast_to(row, (LANES, row.shape[1])).T


def prepare(weights, vectors):
    features, hidden_width = weights[0].shape
    places = weight_places(features, hidden_width)
    gap = jnp.zeros((features, places[3][0] - places[2][0] - places[2][1]), BF16)
    joined = jnp.concatenate([*weights[:3], gap, weights[3]], axis=1)
    rows_of_vectors = jnp.concatenate(vectors).reshape(-1, LANES)
    turned, columns = pl.pallas_call(
        prepare_kernel,
        out_shape=[
            jax.ShapeDtypeStruct(joined.shape[::-1], BF16),
            jax.ShapeDtypeStruct((rows_of_vectors.size, LANES), F32),
        ],
        in_specs=[VMEM] * 2,
        out_specs=[VMEM] * 2,
        compiler_params=PARAMS,
        name="prepare",
    )(joined, rows_of_vectors)
    return joined, turned, columns


def window_call(core, quads, prepared):
    features = prepared[0].shape[0]
    hidden_width = prepared[2].shape[0] - 8 * features
    tokens = 2 * quads[0].size // features
    rows = grad_rows(features, hidden_width)
    quad = jax.ShapeDtypeStruct((quads[0].shape[0] // 2, quads[0].shape[1]), BF16)
    half = jax.ShapeDtypeStruct((rows // 2, LANES), BF16)
    return pl.pallas_call(
        window_kernel,
        out_shape=[quad] * 4 + [half] * 2,
        in_specs=[SMEM] + [VMEM] * 7,
        out_specs=[VMEM] * 6,
        scratch_shapes=[
            pltpu.VMEM((HEADS, tokens, tokens), BF16),
            pltpu.VMEM((HEADS, tokens, tokens), BF16),
            pltpu.VMEM((3 * features, tokens), F32),
            pltpu.VMEM((rows, LANES), BF16),
        ],
        compiler_params=PARAMS,
        name="window",
    )(core, *quads, *prepared)


def split_kernel(fields_ref, *outs):
    margin = WIN // 2
    fields = [fields_ref[i].astype(F32) for i in range(2)]
    for out, (low_x, low_y) in zip(outs, ((margin, margin), (0, margin), (margin, 0), (0, 0))):
        out[...] = jnp.concatenate(
            [f[low_x + i, low_y : low_y + margin] for f in fields for i in range(margin)], axis=0
        ).astype(BF16)


def split_quarters(tokens, cotangent):
    quad = jax.ShapeDtypeStruct((WIN * WIN // 2, tokens.shape[2]), BF16)
    return pl.pallas_call(
        split_kernel,
        out_shape=[quad] * 4,
        in_specs=[VMEM],
        out_specs=[VMEM] * 4,
        compiler_params=PARAMS,
        name="split",
    )(jnp.stack([tokens, cotangent]))


def join_kernel(*refs):
    margin = WIN // 2
    own, part_x, part_y, part_xy = [ref[...].astype(F32) for ref in refs[:4]]
    out = refs[4]
    for i in range(margin):
        rows = slice(i * margin, (i + 1) * margin)
        out[i] = jnp.concatenate([part_xy[rows], part_x[rows]], axis=0).astype(BF16)
        out[margin + i] = jnp.concatenate([part_y[rows], own[rows]], axis=0).astype(BF16)


def join_quarters(parts):
    return pl.pallas_call(
        join_kernel,
        out_shape=jax.ShapeDtypeStruct((WIN, WIN, parts[0].shape[1]), BF16),
        in_specs=[VMEM] * 4,
        out_specs=VMEM,
        compiler_params=PARAMS,
        name="join",
    )(*parts)


def exchange(steps):
    nx, ny = lax.axis_size("gx"), lax.axis_size("gy")
    ring_x = [(i, (i + steps) % nx) for i in range(nx)]
    ring_y = [(i, (i + steps) % ny) for i in range(ny)]
    both = [
        (i * ny + j, ((i + steps) % nx) * ny + (j + steps) % ny)
        for i in range(nx)
        for j in range(ny)
    ]
    return (
        lambda value: lax.ppermute(value, "gx", ring_x),
        lambda value: lax.ppermute(value, "gy", ring_y),
        lambda value: lax.ppermute(value, BOTH, both),
    )


def swap(value, bit):
    return lax.ppermute(value, BOTH, [(i, i ^ bit) for i in range(256)])


CORE = 16
PLANE = [
    [
        16 * (4 * y + 2 * xh + core) + 8 * xl + 2 * z + zl
        for zl in (0, 1)
        for xh in (0, 1)
        for xl in (0, 1)
        for y in range(4)
    ]
    for core in (0, 1)
    for z in range(4)
]


def sum_everywhere(keep, send, own, sends):
    mine = keep + swap(send, CORE)
    chunk = mine.shape[0] // 32
    pieces = lax.all_to_all(
        mine.reshape(32, chunk, LANES), BOTH, 0, 0, axis_index_groups=PLANE, tiled=True
    )
    received = [move(value) for value, move in zip(sends, exchange(1))]
    grad_tokens = join_quarters([own, *received])
    total = jnp.sum(pieces.astype(F32), axis=0).astype(BF16)
    for bit in (2, 6):
        total = total + swap(total, bit)
    grad_tokens, total = lax.optimization_barrier((grad_tokens, total))
    spread = jnp.broadcast_to(total[None], (32, chunk, LANES))
    whole = lax.all_to_all(spread, BOTH, 0, 0, axis_index_groups=PLANE, tiled=True)
    whole = whole.reshape(-1, LANES)
    return whole, swap(whole, CORE), grad_tokens


def finish_kernel(core, mine, other, o_qkv, o_proj, o_fc1, o_fc2, o_vec, *, factor):
    features, hidden_width = o_fc1.shape
    size = mine.shape[0]

    def unpack(first, second):
        at = 0

        def take(rows):
            nonlocal at
            low, at = at, at + rows
            if at <= size:
                value = first[low:at, :]
            elif low >= size:
                value = second[low - size : at - size, :]
            else:
                value = jnp.concatenate([first[low:, :], second[: at - size, :]], axis=0)
            return value.astype(F32) * factor

        for out in (o_fc1, o_fc2):
            for col in range(0, hidden_width, LANES):
                out[:, col : col + LANES] = take(features)
        both = jnp.concatenate([take(features) for _ in range(4 * features // LANES)], axis=1)
        o_qkv[...] = both[:, : 3 * features]
        o_proj[...] = both[:, 3 * features :]
        o_vec[...] = take(LANES)[: o_vec.shape[0]]

    @pl.when(core[0] == 0)
    def _():
        unpack(mine, other)

    @pl.when(core[0] != 0)
    def _():
        unpack(other, mine)


def finish(core, mine, other, shapes, factor):
    shapes = (*shapes[:3], shapes[3][::-1], (shapes[4] // LANES, LANES))
    outs = [jax.ShapeDtypeStruct(shape, F32) for shape in shapes]
    return pl.pallas_call(
        partial(finish_kernel, factor=factor),
        out_shape=outs,
        in_specs=[SMEM, VMEM, VMEM],
        out_specs=[VMEM] * 5,
        compiler_params=PARAMS,
        name="finish",
    )(core, mine, other)


def on_device(
    tokens, cotangent, qkv_w, qkv_b, proj_w, proj_b, fc1_w, fc1_b, fc2_w, g1, b1, g2, b2
):
    features = g1.shape[0]
    token_count = tokens.size // features * lax.axis_size("gx") * lax.axis_size("gy")
    factor = float(token_count) ** (-0.5)
    core = (lax.axis_index("gx") % 2).astype(jnp.int32).reshape(1)
    vectors = (qkv_b, proj_b, fc1_b, g1, b1, g2, b2)
    own, *sends = split_quarters(tokens, cotangent)
    quads = [own] + [move(value) for value, move in zip(sends, exchange(-1))]
    prepared = prepare((fc1_w, fc2_w.T, qkv_w, proj_w), vectors)
    own, *sends, keep, send = window_call(core, quads, prepared)
    mine, other, grad_tokens = sum_everywhere(keep, send, own, sends)
    shapes = [w.shape for w in (qkv_w, proj_w, fc1_w, fc2_w)] + [sum(v.size for v in vectors)]
    grads = finish(core, mine, other, shapes, factor)
    return (grad_tokens, *grads[:3], grads[3].T, grads[4].reshape(-1))


def solution(mesh):
    spec = P("gx", "gy", None)
    return jax.shard_map(
        on_device,
        mesh=mesh,
        in_specs=(spec, spec) + (P(),) * 11,
        out_specs=(spec,) + (P(),) * 5,
        check_vma=False,
    )
```
